32 devices in a mesh: parts: 2 (over y), lat: 4 (over z), fsdp: 2 (over x), sub: 2 (over core).
Axes of the slice: x: 2, y: 2, z: 4, core: 2. Of those that a mesh axis runs over, the one named last changes fastest.
Arguments:
- grid_input_channels: bfloat16 [8, 2, 227, 4096], P(('parts', 'lat'), 'sub', None, 'fsdp'), parts along dimension 0, may hold values from -6 to 6
- cotangent: bfloat16 [8, 2, 512, 4096], P(('parts', 'lat'), 'sub', 'fsdp'), parts along dimension 0
- frozen_input_weight: bfloat16 [227, 512], replicated, may hold values from -0.375 to 0.375
- frozen_output_weight: bfloat16 [512, 512], replicated, may hold values from -0.25 to 0.25
- adapter_down_weight: bfloat16 [454, 16], P('parts'), parts along dimension 0, may hold values from -0.375 to 0.375
- adapter_up_weight: bfloat16 [32, 512], P('parts'), parts along dimension 0, may hold values from -1.5 to 1.5
- interp: bfloat16 [4, 2, 96, 128, 128], P('lat', 'sub'), may hold values from -0.1875 to 0.1875
- nonzero_block_rows: int32 [4, 2, 96], P('lat', 'sub'), may hold values from 0 to 11, as said below
- nonzero_block_columns: int32 [4, 2, 96], P('lat', 'sub'), may hold values from 0 to 255, as said below
- grid_block_storage: int32 [256], replicated, may hold values from 0 to 255, as said below
Outputs:
- decoded: bfloat16 [8, 2, 512, 4096], P(('parts', 'lat'), 'sub', 'fsdp'), parts along dimension 0
- grad_down: float32 [454, 16], P('parts'), parts along dimension 0
- up_gradient: float32 [32, 512], P('parts'), parts along dimension 0
The draws below stay inside these ranges and needn't reach their ends.
There are 2 independent parts, one for each index of `parts`. The reference program is written for one: setup_inputs(seed, part) draws one part's arguments, and reference() takes and returns one part's arrays. A program takes and returns all parts, laid end to end along the dimension named above; an argument that names none is the same for every part. Nothing has to cross between parts.
Inputs may be any that keep to these rules, and one draw needn't show every extreme that they name: Each number once; grid block b is stored as block grid_block_storage[b] % 32 of tile half grid_block_storage[b] // 32. `nonzero_block_columns`: within each tile half, at most 16 slots read grid blocks stored by any one tile half; in every draw exactly 16 slots of every tile half read grid blocks stored by one and the same tile half. `nonzero_block_rows`: within each tile half every mesh block has exactly 8 slots.
All inputs are finite; a program needn't handle non-finite values.
Results may differ from the reference program's by a relative error of at most 0.0083.
Values may be sent and summed in bfloat16 or wider, within the bound.
No kernel may reach another device: no remote copies, remote signals or barrier semaphores. Data moves between devices by JAX's collectives and lax.ppermute only.
A program may use at most 192 MiB of HBM per device.

```python
import jax
import jax.numpy as jnp
from jax import lax

INPUT_CHANNELS = 227
LATENT_WIDTH = 512
ADAPTER_RANK = 16
BLK = 128
FANIN = 8
GBLK = 32
MBLK = 12
TILES = 4
HALVES = 2
GROWS = 4096
NBLOCKS = 256
GRID = 32768
SLOTS = 96
CAP = 16


def draw_pattern(key):
    pairs = TILES * HALVES
    spots = pairs * CAP
    key_place, key_full, key_score, key_local = jax.random.split(key, 4)
    grid_block_storage = jax.random.permutation(key_place, pairs * GBLK).astype(jnp.int32)
    full_owner = jax.random.randint(key_full, (), 0, pairs)
    position = jnp.arange(spots, dtype=jnp.int32)
    owner_of = position // CAP
    tile_of = owner_of // HALVES
    polar = ((tile_of == 0) | (tile_of == TILES - 1)).astype(jnp.int32)
    score = jax.random.randint(key_score, (pairs, spots), 0, 1000) + 400 * polar[None, :]
    score = score + 100000 * (owner_of == full_owner).astype(jnp.int32)[None, :]
    score = score * spots + position[None, :]
    chosen = lax.top_k(score, SLOTS)[1]
    owners = chosen // CAP
    local = jax.random.randint(key_local, (pairs, SLOTS), 0, GBLK)
    stored = owners * GBLK + local
    inverse = jnp.argsort(grid_block_storage)
    nonzero_block_columns = inverse[stored].astype(jnp.int32).reshape(TILES, HALVES, SLOTS)
    return (grid_block_storage, nonzero_block_columns)


def draw_grid_block_storage(key, part):
    return draw_pattern(key)[0]


def draw_nonzero_block_columns(key, part):
    return draw_pattern(key)[1]


def shuffled_slots(key):
    return jax.random.permutation(key, SLOTS)


def draw_nonzero_block_rows(key, part):
    key = jax.random.fold_in(key, 3)
    keys = jax.random.split(key, TILES * HALVES)
    orders = jax.vmap(shuffled_slots)(keys)
    return (orders % MBLK).astype(jnp.int32).reshape(TILES, HALVES, SLOTS)


def draw_cotangent(key, part):
    key = jax.random.fold_in(key, 5)
    shape = (TILES, HALVES, LATENT_WIDTH, GROWS)
    pair_index = (jnp.arange(TILES)[:, None] * HALVES + jnp.arange(HALVES)[None, :]).astype(jnp.float32)
    row_index = pair_index[:, :, None, None] * GROWS + jnp.arange(GROWS, dtype=jnp.float32)[None, None, None, :]
    ramp = 1.0 + 2.0 * row_index / GRID
    base = jax.random.normal(key, shape, jnp.float32)
    return (base * ramp * GRID ** (-0.5)).astype(jnp.bfloat16)


def shard_levels(rng, shape, shards, smallest, high):
    level, own = 1.0, jax.random.fold_in(rng, 6)
    for axis_at, shards_of in shards:
        steps = jnp.exp(jax.random.uniform(jax.random.fold_in(own, axis_at), (shards_of,), jnp.float32, smallest / len(shards), high / len(shards)))
        level = level * jnp.repeat(steps, shape[axis_at] // shards_of).reshape([-1 if axis == axis_at else 1 for axis in range(len(shape))])
    return level


def noise(stream_key, extent, width, reach, shards=(), kind=jnp.bfloat16):
    array = width * jax.random.normal(stream_key, extent, jnp.float32)
    if shards:
        array = array * shard_levels(stream_key, extent, shards, -0.22, 0.18)
    return jnp.clip(array, -reach, reach).astype(kind)


def setup_inputs(seed: int = 0, part: int = 0) -> dict:
    key_list = jax.random.split(jax.random.key(seed), 11)
    own_keys = jax.random.split(jax.random.fold_in(key_list[10], part), 11)
    grid_input_channels = noise(own_keys[0], (TILES, HALVES, INPUT_CHANNELS, GROWS), 1.0, 6.0, ((0, 4), (1, 2), (3, 2)))
    cotangent = draw_cotangent(jax.random.fold_in(jax.random.fold_in(key_list[10], part), 71), part)
    frozen_input_weight = noise(key_list[2], (INPUT_CHANNELS, LATENT_WIDTH), INPUT_CHANNELS ** -0.5, 0.375)
    frozen_output_weight = noise(key_list[3], (LATENT_WIDTH, LATENT_WIDTH), LATENT_WIDTH ** -0.5, 0.25)
    adapter_down_weight = noise(own_keys[4], (INPUT_CHANNELS, ADAPTER_RANK), INPUT_CHANNELS ** -0.5, 0.375)
    adapter_up_weight = noise(own_keys[5], (ADAPTER_RANK, LATENT_WIDTH), ADAPTER_RANK ** -0.5, 1.5)
    interp = noise(key_list[6], (TILES, HALVES, SLOTS, BLK, BLK), (BLK * FANIN) ** -0.5, 0.1875, ((0, 4), (1, 2)))
    nonzero_block_rows = draw_nonzero_block_rows(jax.random.fold_in(key_list[10], 71), part)
    nonzero_block_columns = draw_nonzero_block_columns(jax.random.fold_in(key_list[10], 71), part)
    grid_block_storage = draw_grid_block_storage(jax.random.fold_in(key_list[10], 71), part)
    return dict(grid_input_channels=grid_input_channels, cotangent=cotangent, frozen_input_weight=frozen_input_weight, frozen_output_weight=frozen_output_weight, adapter_down_weight=adapter_down_weight, adapter_up_weight=adapter_up_weight, interp=interp, nonzero_block_rows=nonzero_block_rows, nonzero_block_columns=nonzero_block_columns, grid_block_storage=grid_block_storage)


def encode(blocks, values, places, rows):

    def one_half(inputs):
        block_vals, block_places, block_rows_here = inputs
        panels = blocks[block_places].astype(jnp.float32)
        products = jnp.einsum('kmi,kic->kmc', block_vals.astype(jnp.float32), panels, precision=lax.Precision.HIGHEST)
        row_marks = (block_rows_here[:, None] == jnp.arange(MBLK, dtype=jnp.int32)[None, :]).astype(jnp.float32)
        summed = jnp.einsum('kr,kmc->rmc', row_marks, products, precision=lax.Precision.HIGHEST)
        return summed.astype(jnp.bfloat16)
    return lax.map(one_half, (values, places, rows))

def adjoint(mesh_blocks, values, places, rows):

    def one_half(total, inputs):
        block_vals, block_places, block_rows_here, mesh_here = inputs
        picked = mesh_here[block_rows_here].astype(jnp.float32)
        contrib = jnp.einsum('kmi,kmc->kic', block_vals.astype(jnp.float32), picked, precision=lax.Precision.HIGHEST)
        contrib = contrib.astype(jnp.bfloat16).astype(jnp.float32)
        return (total.at[block_places].add(contrib), None)
    start = jnp.zeros((NBLOCKS, BLK, LATENT_WIDTH), jnp.float32)
    total, _ = lax.scan(one_half, start, (values, places, rows, mesh_blocks))
    return total.astype(jnp.bfloat16)

def reference(grid_input_channels, cotangent, frozen_input_weight, frozen_output_weight, adapter_down_weight, adapter_up_weight, interp, nonzero_block_rows, nonzero_block_columns, grid_block_storage):
    pairs = TILES * HALVES
    feature_rows = jnp.transpose(grid_input_channels, (0, 1, 3, 2)).reshape(GRID, INPUT_CHANNELS)
    adapter_middle_state = jnp.dot(feature_rows, adapter_down_weight, preferred_element_type=jnp.float32).astype(jnp.bfloat16)
    preactivation_values = jnp.dot(feature_rows, frozen_input_weight, preferred_element_type=jnp.float32) + jnp.dot(adapter_middle_state, adapter_up_weight, preferred_element_type=jnp.float32)
    hidden = jax.nn.silu(preactivation_values).astype(jnp.bfloat16)
    raw_out = jnp.dot(hidden, frozen_output_weight, preferred_element_type=jnp.float32)
    center = raw_out - lax.optimization_barrier(jnp.mean(raw_out, axis=1, keepdims=True))
    inv_std = lax.rsqrt(lax.optimization_barrier(jnp.mean(center * center, axis=1, keepdims=True)) + 1e-05)
    normed = center * inv_std
    embedded = normed.astype(jnp.bfloat16)
    places = grid_block_storage[nonzero_block_columns.reshape(pairs, SLOTS)].astype(jnp.int32)
    rows = nonzero_block_rows.reshape(pairs, SLOTS).astype(jnp.int32)
    values = interp.reshape(pairs, SLOTS, BLK, BLK)
    mesh = encode(embedded.reshape(NBLOCKS, BLK, LATENT_WIDTH), values, places, rows)
    decoded_rows = adjoint(mesh, values, places, rows).reshape(GRID, LATENT_WIDTH)
    decoded = jnp.transpose(decoded_rows.reshape(TILES, HALVES, GROWS, LATENT_WIDTH), (0, 1, 3, 2))
    cot_rows = jnp.transpose(cotangent, (0, 1, 3, 2)).reshape(NBLOCKS, BLK, LATENT_WIDTH)
    mesh_grad = encode(cot_rows, values, places, rows)
    embed_grad = adjoint(mesh_grad, values, places, rows).reshape(GRID, LATENT_WIDTH).astype(jnp.float32)
    raw_grad = inv_std * (embed_grad - lax.optimization_barrier(jnp.mean(embed_grad, axis=1, keepdims=True)) - normed * lax.optimization_barrier(jnp.mean(embed_grad * normed, axis=1, keepdims=True)))
    raw_grad = raw_grad.astype(jnp.bfloat16)
    hidden_grad = jnp.dot(raw_grad, frozen_output_weight.T, preferred_element_type=jnp.float32)
    gate_sig = jax.nn.sigmoid(preactivation_values)
    preactivation_gradient = (hidden_grad * gate_sig * (1.0 + preactivation_values * (1.0 - gate_sig))).astype(jnp.bfloat16)
    up_gradient = jnp.dot(adapter_middle_state.T, preactivation_gradient, preferred_element_type=jnp.float32)
    middle_gradient = jnp.dot(preactivation_gradient, adapter_up_weight.T, preferred_element_type=jnp.float32).astype(jnp.bfloat16)
    grad_down = jnp.dot(feature_rows.T, middle_gradient, preferred_element_type=jnp.float32)
    return (decoded, grad_down, up_gradient)
```

```python
import functools

import jax
import jax.numpy as jnp
from jax import lax
from jax.experimental import pallas as pl
from jax.experimental.pallas import tpu as pltpu
from jax.sharding import PartitionSpec as P

MBLK = 12
BF = jnp.bfloat16
F32 = jnp.float32
VMEM_LIMIT = 44 * 1024 * 1024


def params(**kw):
    return pltpu.CompilerParams(vmem_limit_bytes=VMEM_LIMIT, **kw)


def dg(a, b, ca, cb):
    return lax.dot_general(a, b, (((ca,), (cb,)), ((), ())), preferred_element_type=F32)


def places_of(storage, cols):
    ids = jnp.arange(storage.shape[0], dtype=jnp.int32)
    return jnp.sum(jnp.where(cols[..., None] == ids, storage, 0), axis=-1)


def ranks_in(mask):
    size = mask.shape[-1]
    before = jnp.arange(size)[:, None] > jnp.arange(size)[None, :]
    return jnp.sum(jnp.where(before, mask[..., None, :], 0), axis=-1)


def pack_kernel(src, interp, *rest):
    outs, sem = rest[:-1], rest[-1]
    pairs, width = outs[0].shape[0], outs[0].shape[1]
    copies = []
    for h, out in enumerate(outs):
        for o in range(pairs):
            for c in range(width):
                copies.append(
                    pltpu.make_async_copy(
                        interp.at[src[o, h * width + c]], out.at[o, c], sem.at[len(copies)]
                    )
                )
    for copy in copies:
        copy.start()
    for copy in copies:
        copy.wait()


def pack(src, values, pieces):
    pairs, width = src.shape[0], src.shape[1] // pieces
    block = values.shape[1]
    return pl.pallas_call(
        pack_kernel,
        grid_spec=pltpu.PrefetchScalarGridSpec(
            num_scalar_prefetch=1,
            grid=(1,),
            in_specs=[pl.BlockSpec(memory_space=pl.ANY)],
            out_specs=[pl.BlockSpec(memory_space=pl.ANY)] * pieces,
            scratch_shapes=[pltpu.SemaphoreType.DMA((pairs * src.shape[1],))],
        ),
        out_shape=[jax.ShapeDtypeStruct((pairs, width, block, block), BF)] * pieces,
        compiler_params=params(),
        name="pack",
    )(src, values)


def forward_kernel(meta, x, w_in, a_down, a_up, w_out, emb, normed, slope, inv, mid, hold):
    feats = x[...]
    middle = dg(a_down[...], feats, 0, 0).astype(BF)
    pre = dg(w_in[...], feats, 0, 0) + dg(a_up[...], middle, 0, 0)
    sig = jax.nn.sigmoid(pre)
    hidden = (pre * sig).astype(BF)
    slope[...] = sig * (1.0 + pre * (1.0 - sig))
    raw = dg(w_out[...], hidden, 0, 0)
    center = raw - jnp.mean(raw, axis=0, keepdims=True)
    istd = lax.rsqrt(jnp.mean(center * center, axis=0, keepdims=True) + 1e-05)
    norm = center * istd
    normed[...] = norm
    inv[...] = istd
    mid[...] = middle
    hold[...] = norm.astype(BF)
    nf, chans = emb.shape[0], emb.shape[1]
    for r in range(nf):
        at = lax.rem(meta[0] + r, nf) * chans
        emb[r] = hold[pl.ds(pl.multiple_of(at, chans), chans), :]


def forward(meta, x, w_in, a_down, a_up, w_out, nf):
    width, rows = w_out.shape[0], x.shape[1]
    rank = a_down.shape[1]
    step = min(512, rows)
    chans = width // nf
    full = lambda a: pl.BlockSpec(a.shape, lambda i, m: (0, 0))
    return pl.pallas_call(
        forward_kernel,
        grid_spec=pltpu.PrefetchScalarGridSpec(
            num_scalar_prefetch=1,
            grid=(rows // step,),
            in_specs=[
                pl.BlockSpec((x.shape[0], step), lambda i, m: (0, i)),
                full(w_in),
                full(a_down),
                full(a_up),
                full(w_out),
            ],
            out_specs=[
                pl.BlockSpec((nf, chans, step), lambda i, m: (0, 0, i)),
                pl.BlockSpec((width, step), lambda i, m: (0, i)),
                pl.BlockSpec((width, step), lambda i, m: (0, i)),
                pl.BlockSpec((1, step), lambda i, m: (0, i)),
                pl.BlockSpec((rank, step), lambda i, m: (0, i)),
            ],
            scratch_shapes=[pltpu.VMEM((width, step), BF)],
        ),
        out_shape=[
            jax.ShapeDtypeStruct((nf, chans, rows), BF),
            jax.ShapeDtypeStruct((width, rows), F32),
            jax.ShapeDtypeStruct((width, rows), F32),
            jax.ShapeDtypeStruct((1, rows), F32),
            jax.ShapeDtypeStruct((rank, rows), BF),
        ],
        compiler_params=params(),
        cost_estimate=pl.CostEstimate(
            flops=2 * rows * width * (width + x.shape[0]), bytes_accessed=rows * width * 12, transcendentals=0
        ),
        name="forward",
    )(meta, x, w_in, a_down, a_up, w_out)


def backward_kernel(offs, *refs, count):
    pieces = refs[:count]
    normed, slope, inv, mid, x, w_out, a_up, up, down, hold = refs[count:]
    chans = pieces[0].shape[0]
    for i, piece in enumerate(pieces):
        hold[pl.ds(pl.multiple_of(offs[i], chans), chans), :] = piece[...].astype(F32)
    e = hold[...]
    norm = normed[...]
    raw = inv[...] * (
        e
        - jnp.mean(e, axis=0, keepdims=True)
        - norm * jnp.mean(e * norm, axis=0, keepdims=True)
    )
    hidden_grad = dg(w_out[...], raw.astype(BF), 1, 0)
    pre_grad = (hidden_grad * slope[...]).astype(BF)
    up_term = dg(mid[...], pre_grad, 1, 1)
    mid_grad = dg(a_up[...], pre_grad, 1, 0).astype(BF)
    down_term = dg(mid_grad, x[...], 1, 1)

    @pl.when(pl.program_id(0) == 0)
    def _():
        up[...] = jnp.zeros_like(up)
        down[...] = jnp.zeros_like(down)

    up[...] += up_term
    down[...] += down_term


def backward(offs, pieces, normed, slope, inv, mid, x, w_out, a_up):
    width, rows = normed.shape
    rank = a_up.shape[0]
    step = min(512, rows)
    full = lambda a: pl.BlockSpec(a.shape, lambda i, m: (0, 0))
    tall = lambda a: pl.BlockSpec((a.shape[0], step), lambda i, m: (0, i))
    return pl.pallas_call(
        functools.partial(backward_kernel, count=len(pieces)),
        grid_spec=pltpu.PrefetchScalarGridSpec(
            num_scalar_prefetch=1,
            grid=(rows // step,),
            in_specs=[tall(p) for p in pieces]
            + [tall(normed), tall(slope), tall(inv), tall(mid), tall(x), full(w_out), full(a_up)],
            out_specs=[
                pl.BlockSpec((rank, width), lambda i, m: (0, 0)),
                pl.BlockSpec((rank, x.shape[0]), lambda i, m: (0, 0)),
            ],
            scratch_shapes=[pltpu.VMEM((width, step), F32)],
        ),
        out_shape=[
            jax.ShapeDtypeStruct((rank, width), F32),
            jax.ShapeDtypeStruct((rank, x.shape[0]), F32),
        ],
        compiler_params=params(),
        cost_estimate=pl.CostEstimate(
            flops=2 * rows * width * width, bytes_accessed=rows * width * 10, transcendentals=0
        ),
        name="backward",
    )(offs, *pieces, normed, slope, inv, mid, x, w_out, a_up)


def encode_kernel(tab_j, tab_m, meta, *refs, panels, weights, n, ns):
    xs, ws = refs[:panels], refs[panels : panels + weights]
    out, acc = refs[panels + weights], refs[panels + weights + 1]
    r = pl.program_id(0)
    p = lax.rem(meta[0] + r, n) * ns + meta[1]
    block = out.shape[3]
    if panels > 1:
        hold = refs[panels + weights + 2]
        wide = xs[0].shape[1]

        @pl.when(r == 0)
        def _():
            for i, piece in enumerate(xs):
                at = lax.rem(meta[2] + panels - i, panels) * wide
                hold[:, pl.ds(pl.multiple_of(at, wide), wide)] = piece[...]

        source = hold
    else:
        source = xs[0]
    acc[...] = jnp.zeros_like(acc)
    slot = 0
    for w in ws:
        for c in range(w.shape[1]):
            j, m = tab_j[p, slot], tab_m[p, slot]
            slot += 1
            panel = source[:, pl.ds(pl.multiple_of(j * block, block), block)]
            acc[m] += dg(panel, w[0, c], 1, 1)
    out[0] = acc[0 : out.shape[1]].astype(BF)


def encode(tab_j, tab_m, meta, pieces, chunk, chunks, weights, n, ns):
    chans, wide = pieces[0].shape[0] // chunks, pieces[0].shape[1]
    panels = len(pieces)
    block = weights[0].shape[2]
    cap = sum(w.shape[1] for w in weights)
    scratch = [pltpu.VMEM((MBLK + 1, chans, block), F32)]
    if panels > 1:
        scratch.append(pltpu.VMEM((chans, wide * panels), BF))
    where = lambda r, j, m, t: (lax.rem(t[0] + r, n) * ns + t[1], 0, 0, 0)
    return pl.pallas_call(
        functools.partial(encode_kernel, panels=panels, weights=len(weights), n=n, ns=ns),
        grid_spec=pltpu.PrefetchScalarGridSpec(
            num_scalar_prefetch=3,
            grid=(n,),
            in_specs=[pl.BlockSpec((chans, wide), lambda r, j, m, t: (chunk, 0))] * panels
            + [pl.BlockSpec((1,) + w.shape[1:], where) for w in weights],
            out_specs=pl.BlockSpec((1, MBLK, chans, block), lambda r, j, m, t: (r, 0, 0, 0)),
            scratch_shapes=scratch,
        ),
        out_shape=jax.ShapeDtypeStruct((n, MBLK, chans, block), BF),
        compiler_params=params(),
        cost_estimate=pl.CostEstimate(
            flops=2 * n * cap * chans * block * block * 4,
            bytes_accessed=n * MBLK * chans * block * 4,
            transcendentals=0,
        ),
        name="encode",
    )(tab_j, tab_m, meta, *pieces, *weights)


def decode_kernel(tab_j, tab_m, meta, *refs, n, ns, weights, alias, split):
    count = 2 * n - 1
    mine, theirs = refs[:count], refs[count : 2 * count]
    ws = refs[2 * count : 2 * count + weights]
    rest = refs[2 * count + weights + (1 if alias else 0) :]
    out, hold, acc, sem = rest
    z, s = meta[0], meta[1]
    block = hold.shape[3]

    def copies(side, group, go):
        for r in range(n):
            at = r * ns + side
            if r == 0:
                go(pltpu.make_async_copy(group[0], hold.at[at], sem.at[at]))
                continue
            below, above = group[n - r], group[n - 1 + r]

            @pl.when(z + r < n)
            def _():
                go(pltpu.make_async_copy(above, hold.at[at], sem.at[at]))

            @pl.when(z + r >= n)
            def _():
                go(pltpu.make_async_copy(below, hold.at[at], sem.at[at]))

    for side, group in enumerate((mine, theirs)):
        copies(side, group, lambda c: c.start())
    acc[...] = jnp.zeros_like(acc)

    def step(i, carry):
        r, side = i // ns, lax.rem(i, ns)
        p = lax.rem(z + r, n) * ns + lax.rem(s + side, ns)
        pltpu.make_async_copy(mine[0], hold.at[i], sem.at[i]).wait()
        slot = 0
        for w in ws:
            for c in range(w.shape[1]):
                j, m = tab_j[p, slot], tab_m[p, slot]
                slot += 1
                acc[j] += dg(hold[i, jnp.minimum(m, MBLK - 1)], w[p, c], 1, 0)
        return carry

    lax.fori_loop(0, n * ns, step, 0)
    for g in range(acc.shape[0] - 1):
        if split:
            per = out.shape[2] // block
            to = lax.rem(g // per - meta[2] + out.shape[0], out.shape[0])
            out[to, :, (g % per) * block : (g % per + 1) * block] = acc[g].astype(BF)
        else:
            out[:, g * block : (g + 1) * block] = acc[g].astype(BF)


def decode(tab_j, tab_m, meta, mine, theirs, weights, grid_count, chunk, chunks, base, nf, n, ns):
    chans, block = mine[0].shape[1], mine[0].shape[2]
    rows = grid_count * block
    split = nf is not None
    if split:
        shape = (nf, chans, rows // nf)
        out_spec = pl.BlockSpec(shape, lambda i, j, m, t: (0, 0, 0))
    else:
        shape = (chans * chunks, rows)
        out_spec = pl.BlockSpec((chans, rows), lambda i, j, m, t: (chunk, 0))
    alias = base is not None
    count = 2 * len(mine)
    return pl.pallas_call(
        functools.partial(
            decode_kernel, n=n, ns=ns, weights=len(weights), alias=alias, split=split
        ),
        grid_spec=pltpu.PrefetchScalarGridSpec(
            num_scalar_prefetch=3,
            grid=(1,),
            in_specs=[pl.BlockSpec(memory_space=pl.ANY)] * count
            + [pl.BlockSpec(w.shape, lambda i, j, m, t: (0, 0, 0, 0)) for w in weights]
            + ([pl.BlockSpec(memory_space=pl.ANY)] if alias else []),
            out_specs=out_spec,
            scratch_shapes=[
                pltpu.VMEM((n * ns, MBLK, chans, block), BF),
                pltpu.VMEM((grid_count + 1, chans, block), F32),
                pltpu.SemaphoreType.DMA((n * ns,)),
            ],
        ),
        out_shape=jax.ShapeDtypeStruct(shape, BF),
        input_output_aliases={3 + count + len(weights): 0} if alias else {},
        compiler_params=params(),
        cost_estimate=pl.CostEstimate(
            flops=2 * n * ns * 16 * chans * block * block * 4,
            bytes_accessed=2 * n * MBLK * chans * block * 4,
            transcendentals=0,
        ),
        name="decode",
    )(tab_j, tab_m, meta, *mine, *theirs, *weights, *([base] if alias else []))


def total(*terms):
    out = terms[0].astype(F32)
    for term in terms[1:]:
        out = out + term.astype(F32)
    return out.astype(BF)


def swap_sub(a):
    ns = lax.axis_size("sub")
    return lax.ppermute(a, "sub", [(i, (i + 1) % ns) for i in range(ns)])


def reduce_line(own, other):
    n = own.shape[0]
    up = down = None
    for t in range(1, n):
        ups = [own[n - t], other[n - t]] + ([up] if up is not None else [])
        downs = [own[t], other[t]] + ([down] if down is not None else [])
        up = lax.ppermute(total(*ups), "lat", [(i, i + 1) for i in range(n - 1) if i <= t - 1])
        down = lax.ppermute(
            total(*downs), "lat", [(i, i - 1) for i in range(1, n) if i >= n - t]
        )
    return total(own[0], other[0], up, down)


def spread_line(block):
    n = lax.axis_size("lat")
    ups, downs = [block], [block]
    for t in range(1, n):
        ups.append(
            lax.ppermute(ups[-1], "lat", [(i, i + 1) for i in range(n - 1) if i >= t - 1])
        )
        downs.append(lax.ppermute(downs[-1], "lat", [(i, i - 1) for i in range(1, n) if i <= n - t]))
    return ups + downs[1:]


def add_all(value, axes):
    for axis in axes:
        size, step = lax.axis_size(axis), 1
        while step < size:
            value = value + lax.ppermute(value, axis, [(i, i ^ step) for i in range(size)])
            step *= 2
    return value


def body(
    grid_input_channels,
    cotangent,
    frozen_input_weight,
    frozen_output_weight,
    adapter_down_weight,
    adapter_up_weight,
    interp,
    nonzero_block_rows,
    nonzero_block_columns,
    grid_block_storage,
):
    n, ns = lax.axis_size("lat"), lax.axis_size("sub")
    nf, npart = lax.axis_size("fsdp"), lax.axis_size("parts")
    z, s = lax.axis_index("lat"), lax.axis_index("sub")
    f, y = lax.axis_index("fsdp"), lax.axis_index("parts")
    pairs = n * ns
    me = z * ns + s
    slots, block = interp.shape[2], interp.shape[3]
    chans, grid_rows = cotangent.shape[2], cotangent.shape[3]
    grid_count = grid_rows // block
    width = frozen_output_weight.shape[0]
    cap = max(2, (4 * slots + 3 * pairs - 1) // (3 * pairs))
    x = grid_input_channels.reshape(grid_input_channels.shape[2:])
    cot = cotangent.reshape(chans, grid_rows)
    values = interp.reshape(slots, block, block)
    storage = grid_block_storage.astype(jnp.int32)
    cols = nonzero_block_columns.reshape(slots)
    rows = nonzero_block_rows.reshape(slots)
    pair_ids = jnp.arange(pairs, dtype=jnp.int32)

    place = places_of(storage, cols)
    marks = (place[None, :] // grid_count == pair_ids[:, None]).astype(jnp.int32)
    rank = ranks_in(marks)
    shared = nf == 2 and npart == 2 and cap % 8 == 0
    if shared:
        r0 = y * 2 + f
        cs = cap // 4
        send_ranks = r0 * cs + jnp.arange(cs, dtype=jnp.int32)
    else:
        send_ranks = jnp.arange(cap, dtype=jnp.int32)
    hit = (rank[:, None, :] == send_ranks[None, :, None]) & (marks[:, None, :] > 0)
    src = jnp.sum(jnp.where(hit, jnp.arange(slots, dtype=jnp.int32), 0), axis=-1)
    a2a = lambda v: lax.all_to_all(v, ("lat", "sub"), 0, 0, tiled=True)
    if shared:
        first, second = pack(src, values, 2)
        first, second = a2a(first), a2a(second)
        flip = [(0, 1), (1, 0)]
        over_x = lambda v: lax.ppermute(v, "fsdp", flip)
        over_y = lambda v: lax.ppermute(v, "parts", flip)
        x1, y1, x2, y2 = over_x(first), over_y(first), over_x(second), over_y(second)
        weights = [first, second, x1, x2, y1, y2, over_x(y1), over_y(x2)]
        half = jnp.arange(cs, dtype=jnp.int32)
        slot_ranks = jnp.concatenate([(r0 ^ k) * cs + half for k in range(4)])
    else:
        weights = [a2a(pack(src, values, 1)[0])]
        slot_ranks = send_ranks

    both = lax.all_gather(jnp.stack([cols, rows])[None], ("lat", "sub"), tiled=True)
    every = places_of(storage, both[:, 0])
    mine = (every // grid_count == me).astype(jnp.int32)
    mine_rank = ranks_in(mine)
    hit = (mine_rank[:, None, :] == slot_ranks[None, :, None]) & (mine[:, None, :] > 0)
    found = jnp.any(hit, axis=-1)
    local = jnp.sum(jnp.where(hit, (every % grid_count)[:, None, :], 0), axis=-1)
    tab_m = jnp.where(found, jnp.sum(jnp.where(hit, both[:, 1][:, None, :], 0), axis=-1), MBLK)
    tab_get = jnp.where(found, local, 0)
    tab_put = jnp.where(found, local, grid_count)

    meta_f = jnp.stack([f]).astype(jnp.int32)
    emb, normed, slope, inv, mid = forward(
        meta_f, x, frozen_input_weight, adapter_down_weight, adapter_up_weight,
        frozen_output_weight, nf,
    )
    shift = lambda v, r: lax.ppermute(v, "fsdp", [(i, (i + r) % nf) for i in range(nf)])
    emb_pieces = [emb[r] if r == 0 else shift(emb[r], r) for r in range(nf)]

    meta_own = jnp.stack([z, s, f]).astype(jnp.int32)
    meta_sib = jnp.stack([z, (s + 1) % ns, f]).astype(jnp.int32)
    chunks = 2

    def mesh_of(pieces, chunk):
        args = (pieces, chunk, chunks, weights, n, ns)
        other = swap_sub(encode(tab_get, tab_m, meta_sib, *args))
        own = encode(tab_get, tab_m, meta_own, *args)
        return reduce_line(own, other)

    def grid_of(mesh, chunk, base, split):
        here = spread_line(mesh)
        there = [swap_sub(a) for a in here]
        return decode(
            tab_put, tab_m, meta_own, here, there, weights, grid_count, chunk, chunks, base,
            nf if split else None, n, ns,
        )

    cot_mesh = [mesh_of([cot], c) for c in range(chunks)]
    emb_mesh = [mesh_of(emb_pieces, c) for c in range(chunks)]
    grads, offs = [], []
    for c in range(chunks):
        grad = grid_of(cot_mesh[c], c, None, True)
        for r in range(nf):
            grads.append(grad[r] if r == 0 else shift(grad[r], r))
            offs.append(((f - r + nf) % nf) * chans + c * (chans // chunks))
    decoded = None
    for c in range(chunks):
        decoded = grid_of(emb_mesh[c], c, decoded, False)

    up, down = backward(
        jnp.stack(offs).astype(jnp.int32), grads, normed, slope, inv, mid, x,
        frozen_output_weight, adapter_up_weight,
    )
    sums = add_all(jnp.concatenate([up, down], axis=1), ("sub", "fsdp", "lat"))
    up_gradient, grad_down = sums[:, :width], sums[:, width:].T
    return (decoded.reshape(1, 1, chans, grid_rows), grad_down, up_gradient)


def solution(mesh):
    in_specs = (
        P(("parts", "lat"), "sub", None, "fsdp"),
        P(("parts", "lat"), "sub", "fsdp", None),
        P(),
        P(),
        P("parts", None),
        P("parts", None),
        P("lat", "sub", None, None, None),
        P("lat", "sub", None),
        P("lat", "sub", None),
        P(),
    )
    out_specs = (P(("parts", "lat"), "sub", "fsdp", None), P("parts", None), P("parts", None))
    return jax.shard_map(body, mesh=mesh, in_specs=in_specs, out_specs=out_specs, check_vma=False)
```

```python
import functools

import jax
import jax.numpy as jnp
from jax import lax
from jax.experimental import pallas as pl
from jax.experimental.pallas import tpu as pltpu
from jax.sharding import PartitionSpec as P

MBLK = 12
BF = jnp.bfloat16
F32 = jnp.float32
VMEM_LIMIT = 28 * 1024 * 1024


def params(**kw):
    return pltpu.CompilerParams(vmem_limit_bytes=VMEM_LIMIT, **kw)


def dg(a, b, ca, cb):
    return lax.dot_general(a, b, (((ca,), (cb,)), ((), ())), preferred_element_type=F32)


def places_of(storage, cols):
    ids = jnp.arange(storage.shape[0], dtype=jnp.int32)
    return jnp.sum(jnp.where(cols[..., None] == ids, storage, 0), axis=-1)


def ranks_in(mask):
    size = mask.shape[-1]
    before = jnp.arange(size)[:, None] > jnp.arange(size)[None, :]
    return jnp.sum(jnp.where(before, mask[..., None, :], 0), axis=-1)


def pack_kernel(src, interp, *outs):
    pairs, width = outs[0].shape[0], outs[0].shape[1]
    for h, out in enumerate(outs):
        for o in range(pairs):
            for c in range(width):
                out[o, c] = interp[src[o, h * width + c]]


def pack(src, values, pieces):
    pairs, width = src.shape[0], src.shape[1] // pieces
    block = values.shape[1]
    shape = (pairs, width, block, block)
    return pl.pallas_call(
        pack_kernel,
        grid_spec=pltpu.PrefetchScalarGridSpec(
            num_scalar_prefetch=1,
            grid=(1,),
            in_specs=[pl.BlockSpec(values.shape, lambda i, t: (0, 0, 0))],
            out_specs=[pl.BlockSpec(shape, lambda i, t: (0, 0, 0, 0))] * pieces,
        ),
        out_shape=[jax.ShapeDtypeStruct(shape, BF)] * pieces,
        compiler_params=params(),
        name="pack",
    )(src, values)


def forward_kernel(meta, x, w_in, a_down, a_up, w_out, *rest, nf, deps):
    embs, rest = rest[deps : deps + nf], rest[deps + nf :]
    normed, slope, inv, mid, hold = rest
    feats = x[...]
    middle = dg(a_down[...], feats, 0, 0).astype(BF)
    pre = dg(w_in[...], feats, 0, 0) + dg(a_up[...], middle, 0, 0)
    sig = jax.nn.sigmoid(pre)
    hidden = (pre * sig).astype(BF)
    slope[...] = sig * (1.0 + pre * (1.0 - sig))
    raw = dg(w_out[...], hidden, 0, 0)
    center = raw - jnp.mean(raw, axis=0, keepdims=True)
    istd = lax.rsqrt(jnp.mean(center * center, axis=0, keepdims=True) + 1e-05)
    norm = center * istd
    normed[...] = norm
    inv[...] = istd
    mid[...] = middle
    hold[...] = norm.astype(BF)
    chans = embs[0].shape[0]
    for r, emb in enumerate(embs):
        at = lax.rem(meta[0] + r, nf) * chans
        emb[...] = hold[pl.ds(pl.multiple_of(at, chans), chans), :]


def forward(meta, x, w_in, a_down, a_up, w_out, nf, deps):
    width, rows = w_out.shape[0], x.shape[1]
    rank = a_down.shape[1]
    step = min(512, rows)
    chans = width // nf
    full = lambda a: pl.BlockSpec(a.shape, lambda i, m: (0, 0))
    return pl.pallas_call(
        functools.partial(forward_kernel, nf=nf, deps=len(deps)),
        grid_spec=pltpu.PrefetchScalarGridSpec(
            num_scalar_prefetch=1,
            grid=(rows // step,),
            in_specs=[
                pl.BlockSpec((x.shape[0], step), lambda i, m: (0, i)),
                full(w_in),
                full(a_down),
                full(a_up),
                full(w_out),
            ]
            + [pl.BlockSpec(memory_space=pl.ANY)] * len(deps),
            out_specs=[pl.BlockSpec((chans, step), lambda i, m: (0, i))] * nf
            + [
                pl.BlockSpec((width, step), lambda i, m: (0, i)),
                pl.BlockSpec((width, step), lambda i, m: (0, i)),
                pl.BlockSpec((1, step), lambda i, m: (0, i)),
                pl.BlockSpec((rank, step), lambda i, m: (0, i)),
            ],
            scratch_shapes=[pltpu.VMEM((width, step), BF)],
        ),
        out_shape=[jax.ShapeDtypeStruct((chans, rows), BF)] * nf
        + [
            jax.ShapeDtypeStruct((width, rows), F32),
            jax.ShapeDtypeStruct((width, rows), F32),
            jax.ShapeDtypeStruct((1, rows), F32),
            jax.ShapeDtypeStruct((rank, rows), BF),
        ],
        compiler_params=params(),
        cost_estimate=pl.CostEstimate(
            flops=2 * rows * width * (width + x.shape[0]), bytes_accessed=rows * width * 12, transcendentals=0
        ),
        name="forward",
    )(meta, x, w_in, a_down, a_up, w_out, *deps)


def backward_kernel(offs, *refs, count):
    pieces = refs[:count]
    normed, slope, inv, mid, x, w_out, a_up, up, down, hold = refs[count:]
    chans = pieces[0].shape[0]
    for i, piece in enumerate(pieces):
        hold[pl.ds(pl.multiple_of(offs[i], chans), chans), :] = piece[...].astype(F32)
    e = hold[...]
    norm = normed[...]
    raw = inv[...] * (
        e
        - jnp.mean(e, axis=0, keepdims=True)
        - norm * jnp.mean(e * norm, axis=0, keepdims=True)
    )
    hidden_grad = dg(w_out[...], raw.astype(BF), 1, 0)
    pre_grad = (hidden_grad * slope[...]).astype(BF)
    up_term = dg(mid[...], pre_grad, 1, 1)
    mid_grad = dg(a_up[...], pre_grad, 1, 0).astype(BF)
    down_term = dg(mid_grad, x[...], 1, 1)

    @pl.when(pl.program_id(0) == 0)
    def _():
        up[...] = jnp.zeros_like(up)
        down[...] = jnp.zeros_like(down)

    up[...] += up_term
    down[...] += down_term


def backward(offs, pieces, normed, slope, inv, mid, x, w_out, a_up):
    width, rows = normed.shape
    rank = a_up.shape[0]
    step = min(512, rows)
    full = lambda a: pl.BlockSpec(a.shape, lambda i, m: (0, 0))
    tall = lambda a: pl.BlockSpec((a.shape[0], step), lambda i, m: (0, i))
    return pl.pallas_call(
        functools.partial(backward_kernel, count=len(pieces)),
        grid_spec=pltpu.PrefetchScalarGridSpec(
            num_scalar_prefetch=1,
            grid=(rows // step,),
            in_specs=[tall(p) for p in pieces]
            + [tall(normed), tall(slope), tall(inv), tall(mid), tall(x), full(w_out), full(a_up)],
            out_specs=[
                pl.BlockSpec((rank, width), lambda i, m: (0, 0)),
                pl.BlockSpec((rank, x.shape[0]), lambda i, m: (0, 0)),
            ],
            scratch_shapes=[pltpu.VMEM((width, step), F32)],
        ),
        out_shape=[
            jax.ShapeDtypeStruct((rank, width), F32),
            jax.ShapeDtypeStruct((rank, x.shape[0]), F32),
        ],
        compiler_params=params(),
        cost_estimate=pl.CostEstimate(
            flops=2 * rows * width * width, bytes_accessed=rows * width * 10, transcendentals=0
        ),
        name="backward",
    )(offs, *pieces, normed, slope, inv, mid, x, w_out, a_up)


def encode_kernel(tab_j, tab_m, meta, *refs, panels, weights, deps, n, ns):
    xs, ws = refs[:panels], refs[panels : panels + weights]
    refs = refs[: panels + weights] + refs[panels + weights + deps :]
    out, acc = refs[panels + weights], refs[panels + weights + 1]
    r = pl.program_id(0)
    p = lax.rem(meta[0] + r, n) * ns + meta[1]
    block = out.shape[3]
    if panels > 1:
        hold = refs[panels + weights + 2]
        wide = xs[0].shape[1]

        @pl.when(r == 0)
        def _():
            for i, piece in enumerate(xs):
                at = lax.rem(meta[2] + panels - i, panels) * wide
                hold[:, pl.ds(pl.multiple_of(at, wide), wide)] = piece[...]

        source = hold
    else:
        source = xs[0]
    acc[...] = jnp.zeros_like(acc)
    slot = 0
    for w in ws:
        for c in range(w.shape[1]):
            j, m = tab_j[p, slot], tab_m[p, slot]
            slot += 1
            panel = source[:, pl.ds(pl.multiple_of(j * block, block), block)]
            acc[m] += dg(panel, w[0, c], 1, 1)
    out[0] = acc[0 : out.shape[1]].astype(BF)


def encode(tab_j, tab_m, meta, pieces, chunk, chunks, weights, deps, n, ns):
    chans, wide = pieces[0].shape[0] // chunks, pieces[0].shape[1]
    panels = len(pieces)
    block = weights[0].shape[2]
    cap = sum(w.shape[1] for w in weights)
    scratch = [pltpu.VMEM((MBLK + 1, chans, block), F32)]
    if panels > 1:
        scratch.append(pltpu.VMEM((chans, wide * panels), BF))
    where = lambda r, j, m, t: (lax.rem(t[0] + r, n) * ns + t[1], 0, 0, 0)
    return pl.pallas_call(
        functools.partial(
            encode_kernel, panels=panels, weights=len(weights), deps=len(deps), n=n, ns=ns
        ),
        grid_spec=pltpu.PrefetchScalarGridSpec(
            num_scalar_prefetch=3,
            grid=(n,),
            in_specs=[pl.BlockSpec((chans, wide), lambda r, j, m, t: (chunk, 0))] * panels
            + [pl.BlockSpec((1,) + w.shape[1:], where) for w in weights]
            + [pl.BlockSpec(memory_space=pl.ANY)] * len(deps),
            out_specs=pl.BlockSpec((1, MBLK, chans, block), lambda r, j, m, t: (r, 0, 0, 0)),
            scratch_shapes=scratch,
        ),
        out_shape=jax.ShapeDtypeStruct((n, MBLK, chans, block), BF),
        compiler_params=params(),
        cost_estimate=pl.CostEstimate(
            flops=2 * n * cap * chans * block * block * 4,
            bytes_accessed=n * MBLK * chans * block * 4,
            transcendentals=0,
        ),
        name="encode",
    )(tab_j, tab_m, meta, *pieces, *weights, *deps)


def decode_kernel(tab_j, tab_m, meta, *refs, n, ns, weights, alias, nf):
    here, there, refs = refs[:n], refs[n : 2 * n], refs[2 * n :]
    ws, rest = refs[:weights], refs[weights + (1 if alias else 0) :]
    outs, (hold, acc, sem) = rest[:-3], rest[-3:]
    z, s = meta[0], meta[1]
    block = hold.shape[3]
    for r in range(n):
        for side, mesh in enumerate((here[r], there[r])):
            at = r * ns + side
            pltpu.make_async_copy(mesh, hold.at[at], sem.at[at]).start()
    acc[...] = jnp.zeros_like(acc)

    def step(i, carry):
        p = lax.rem(z + i // ns, n) * ns + lax.rem(s + lax.rem(i, ns), ns)
        pltpu.make_async_copy(here[0], hold.at[i], sem.at[i]).wait()
        slot = 0
        for w in ws:
            for c in range(w.shape[1]):
                j, m = tab_j[p, slot], tab_m[p, slot]
                slot += 1
                acc[j] += dg(hold[i, jnp.minimum(m, MBLK - 1)], w[p, c], 1, 0)
        return carry

    lax.fori_loop(0, n * ns, step, 0)
    per = (acc.shape[0] - 1) // nf
    for r, out in enumerate(outs):
        first = lax.rem(meta[2] + r, nf) * per
        for g in range(per):
            out[:, g * block : (g + 1) * block] = acc[first + g].astype(BF)


def decode(tab_j, tab_m, meta, here, there, weights, grid_count, chunk, chunks, base, nf, n, ns):
    chans, block = here[0].shape[1], here[0].shape[2]
    meshes = [*here, *there]
    rows = grid_count * block
    if nf > 1:
        shape = (chans, rows // nf)
        out_spec = pl.BlockSpec(shape, lambda i, j, m, t: (0, 0))
    else:
        shape = (chans * chunks, rows)
        out_spec = pl.BlockSpec((chans, rows), lambda i, j, m, t: (chunk, 0))
    alias = base is not None
    whole = lambda a: pl.BlockSpec(a.shape, lambda i, j, m, t: (0,) * a.ndim)
    return pl.pallas_call(
        functools.partial(
            decode_kernel, n=n, ns=ns, weights=len(weights), alias=alias, nf=nf
        ),
        grid_spec=pltpu.PrefetchScalarGridSpec(
            num_scalar_prefetch=3,
            grid=(1,),
            in_specs=[pl.BlockSpec(memory_space=pl.ANY)] * len(meshes)
            + [whole(w) for w in weights]
            + ([pl.BlockSpec(memory_space=pl.ANY)] if alias else []),
            out_specs=[out_spec] * nf,
            scratch_shapes=[
                pltpu.VMEM((n * ns, MBLK, chans, block), BF),
                pltpu.VMEM((grid_count + 1, chans, block), F32),
                pltpu.SemaphoreType.DMA((n * ns,)),
            ],
        ),
        out_shape=[jax.ShapeDtypeStruct(shape, BF)] * nf,
        input_output_aliases={3 + 2 * n + len(weights): 0} if alias else {},
        compiler_params=params(),
        cost_estimate=pl.CostEstimate(
            flops=2 * n * ns * 16 * chans * block * block * 4,
            bytes_accessed=2 * n * MBLK * chans * block * 4,
            transcendentals=0,
        ),
        name="decode",
    )(tab_j, tab_m, meta, *meshes, *weights, *([base] if alias else []))


def swap_sub(a):
    ns = lax.axis_size("sub")
    return lax.ppermute(a, "sub", [(i, (i + 1) % ns) for i in range(ns)])


def add_kernel(*refs, terms, deps):
    ins, outs = refs[: sum(terms)], refs[sum(terms) + deps :]
    for out, count in zip(outs, terms):
        value = ins[0][0].astype(F32) + ins[1][0].astype(F32)
        for ref in ins[2:count]:
            value = value + ref[...].astype(F32)
        out[...] = value.astype(BF)
        ins = ins[count:]


def add(own, other, groups, deps):
    shape = own.shape[1:]
    parts = 3 if shape[0] % 3 == 0 else 1
    piece = (shape[0] // parts,) + shape[1:]
    spec = pl.BlockSpec(piece, lambda i: (i, 0, 0))
    arrays, specs = [], []
    for place, terms in groups:
        pick = pl.BlockSpec((1,) + piece, lambda i, place=place: (place, i, 0, 0))
        arrays += [own, other, *terms]
        specs += [pick, pick] + [spec] * len(terms)
    return pl.pallas_call(
        functools.partial(
            add_kernel, terms=[2 + len(terms) for _, terms in groups], deps=len(deps)
        ),
        grid=(parts,),
        in_specs=specs + [pl.BlockSpec(memory_space=pl.ANY)] * len(deps),
        out_specs=[spec] * len(groups),
        out_shape=[jax.ShapeDtypeStruct(shape, BF)] * len(groups),
        compiler_params=params(),
        name="add",
    )(*arrays, *deps)


def reduce_step(t, own, other, up, down, deps):
    n = own.shape[0]
    first = up is None
    up, down = add(
        own, other, [(n - t, [] if first else [up]), (t, [] if first else [down])], deps
    )
    return (
        up,
        lax.ppermute(up, "lat", [(i, i + 1) for i in range(n - 1) if i <= t - 1]),
        lax.ppermute(down, "lat", [(i, i - 1) for i in range(1, n) if i >= n - t]),
    )


def spread_step(t, up, down):
    n = lax.axis_size("lat")
    return (
        lax.ppermute(up, "lat", [(i, i + 1) for i in range(n - 1) if i >= t - 1]),
        lax.ppermute(down, "lat", [(i, i - 1) for i in range(1, n) if i <= n - t]),
    )


def add_all(value, axes):
    for axis in axes:
        size, step = lax.axis_size(axis), 1
        while step < size:
            value = value + lax.ppermute(value, axis, [(i, i ^ step) for i in range(size)])
            step *= 2
    return value


def body(
    grid_input_channels,
    cotangent,
    frozen_input_weight,
    frozen_output_weight,
    adapter_down_weight,
    adapter_up_weight,
    interp,
    nonzero_block_rows,
    nonzero_block_columns,
    grid_block_storage,
):
    n, ns = lax.axis_size("lat"), lax.axis_size("sub")
    nf, npart = lax.axis_size("fsdp"), lax.axis_size("parts")
    z, s = lax.axis_index("lat"), lax.axis_index("sub")
    f, y = lax.axis_index("fsdp"), lax.axis_index("parts")
    pairs = n * ns
    me = z * ns + s
    slots, block = interp.shape[2], interp.shape[3]
    chans, grid_rows = cotangent.shape[2], cotangent.shape[3]
    grid_count = grid_rows // block
    width = frozen_output_weight.shape[0]
    cap = max(2, (4 * slots + 3 * pairs - 1) // (3 * pairs))
    x = grid_input_channels.reshape(grid_input_channels.shape[2:])
    cot = cotangent.reshape(chans, grid_rows)
    values = interp.reshape(slots, block, block)
    storage = grid_block_storage.astype(jnp.int32)
    cols = nonzero_block_columns.reshape(slots)
    rows = nonzero_block_rows.reshape(slots)
    pair_ids = jnp.arange(pairs, dtype=jnp.int32)

    place = places_of(storage, cols)
    marks = (place[None, :] // grid_count == pair_ids[:, None]).astype(jnp.int32)
    rank = ranks_in(marks)
    shared = nf == 2 and npart == 2 and cap % 8 == 0
    if shared:
        r0 = y * 2 + f
        cs = cap // 4
        send_ranks = r0 * cs + jnp.arange(cs, dtype=jnp.int32)
    else:
        send_ranks = jnp.arange(cap, dtype=jnp.int32)
    hit = (rank[:, None, :] == send_ranks[None, :, None]) & (marks[:, None, :] > 0)
    src = jnp.sum(jnp.where(hit, jnp.arange(slots, dtype=jnp.int32), 0), axis=-1)
    a2a = lambda v: lax.all_to_all(v, ("lat", "sub"), 0, 0, tiled=True)
    meta_f = jnp.stack([f]).astype(jnp.int32)
    *emb, normed, slope, inv, mid = forward(
        meta_f, x, frozen_input_weight, adapter_down_weight, adapter_up_weight,
        frozen_output_weight, nf, [],
    )
    if shared:
        first, second = pack(src, values, 2)
        second, _ = lax.optimization_barrier((second, mid))
        first, second = a2a(first), a2a(second)
        flip = [(0, 1), (1, 0)]
        over_x = lambda v: lax.ppermute(v, "fsdp", flip)
        over_y = lambda v: lax.ppermute(v, "parts", flip)
        x1, y1, x2, y2 = over_x(first), over_y(first), over_x(second), over_y(second)
        weights = [first, second, x1, x2, y1, y2, over_x(y1), over_y(x2)]
        half = jnp.arange(cs, dtype=jnp.int32)
        slot_ranks = jnp.concatenate([(r0 ^ k) * cs + half for k in range(4)])
    else:
        weights = [a2a(pack(src, values, 1)[0])]
        slot_ranks = send_ranks

    pattern = jnp.stack([cols, rows])[None]
    if shared:
        pattern, _ = lax.optimization_barrier((pattern, first))
    both = lax.all_gather(pattern, ("lat", "sub"), tiled=True)
    every = places_of(storage, both[:, 0])
    mine = (every // grid_count == me).astype(jnp.int32)
    mine_rank = ranks_in(mine)
    hit = (mine_rank[:, None, :] == slot_ranks[None, :, None]) & (mine[:, None, :] > 0)
    found = jnp.any(hit, axis=-1)
    local = jnp.sum(jnp.where(hit, (every % grid_count)[:, None, :], 0), axis=-1)
    tab_m = jnp.where(found, jnp.sum(jnp.where(hit, both[:, 1][:, None, :], 0), axis=-1), MBLK)
    tab_get = jnp.where(found, local, 0)
    tab_put = jnp.where(found, local, grid_count)

    shift = lambda v, r: lax.ppermute(v, "fsdp", [(i, (i + r) % nf) for i in range(nf)])
    emb_pieces = [emb[r] if r == 0 else shift(emb[r], r) for r in range(nf)]

    meta_own = jnp.stack([z, s, f]).astype(jnp.int32)
    meta_sib = jnp.stack([z, (s + 1) % ns, f]).astype(jnp.int32)
    chunks = 1

    lag = n
    sources = [([cot], c) for c in range(chunks)] + [(emb_pieces, c) for c in range(chunks)]
    state = [{} for _ in sources]
    grads, offs, decoded = [], [], None
    token = mid
    last = lag * (len(sources) - 1) + 2 * (n - 1) + 3
    for now in range(-1, last):
        made, put = [], []

        def keep(where, key, value):
            made.append(value)
            put.append((where, key))

        for k, (pieces, chunk) in enumerate(sources):
            st, at = state[k], now - lag * k
            if at == -1:
                args = (pieces, chunk, chunks, weights, [token], n, ns)
                keep(st, "other", swap_sub(encode(tab_get, tab_m, meta_sib, *args)))
                keep(st, "own", encode(tab_get, tab_m, meta_own, *args))
            elif 0 <= at < n - 1:
                behind = [state[k - 1][key, at + 1] for key in ("up", "down")] if k else []
                sent, up, down = reduce_step(
                    at + 1, st["own"], st["other"], st.get("up"), st.get("down"), behind
                )
                if at == n - 2:
                    token = sent
                keep(st, "up", up)
                keep(st, "down", down)
            elif n - 1 <= at < 2 * n - 2:
                t = at - n + 2
                if t == 1:
                    behind = [state[k - 1]["grad", 0]] if k else []
                    (mesh,) = add(
                        st["own"], st["other"], [(0, [st["up"], st["down"]])], behind
                    )
                    st["here"], st["there"] = {0: mesh}, {0: swap_sub(mesh)}
                    st["up"], st["down"] = mesh, mesh
                if k >= chunks and t > 1:
                    if t == n - 1:
                        sums = backward(
                            jnp.stack(offs).astype(jnp.int32), grads, normed, slope, inv, mid, x,
                            frozen_output_weight, adapter_up_weight,
                        )
                    done = list(sums) if t == n - 1 else grads
                    st["up"], st["down"], *_ = lax.optimization_barrier(
                        (st["up"], st["down"], *done)
                    )
                st["up"], st["down"] = spread_step(t, st["up"], st["down"])
                st["up", t], st["down", t] = st["up"], st["down"]
                for r in range(1, n):
                    if max(r, n - r) == t:
                        st["here"][r] = jnp.where(z + r < n, st["down", r], st["up", n - r])
                        st["there"][r] = swap_sub(st["here"][r])
            elif at == 2 * n - 2:
                grad = k < chunks
                if not grad:
                    sums = add_all(jnp.concatenate(sums, axis=1), ("sub", "fsdp", "lat"))
                    st["here"][0], _ = lax.optimization_barrier((st["here"][0], sums))
                out = decode(
                    tab_put, tab_m, meta_own, [st["here"][r] for r in range(n)],
                    [st["there"][r] for r in range(n)], weights, grid_count,
                    chunk, chunks, None if grad else decoded, nf if grad else 1, n, ns,
                )
                if grad:
                    for r in range(nf):
                        st["grad", r] = out[r]
                else:
                    decoded = out[0]
                if grad:
                    for r in range(nf):
                        piece = st["grad", r]
                        grads.append(piece if r == 0 else shift(piece, r))
                        offs.append(((f - r + nf) % nf) * chans + chunk * (chans // chunks))
        for spot, value in zip(put, made):
            spot[0][spot[1]] = value

    up_gradient, grad_down = sums[:, :width], sums[:, width:].T
    return (decoded.reshape(1, 1, chans, grid_rows), grad_down, up_gradient)


def solution(mesh):
    in_specs = (
        P(("parts", "lat"), "sub", None, "fsdp"),
        P(("parts", "lat"), "sub", "fsdp", None),
        P(),
        P(),
        P("parts", None),
        P("parts", None),
        P("lat", "sub", None, None, None),
        P("lat", "sub", None),
        P("lat", "sub", None),
        P(),
    )
    out_specs = (P(("parts", "lat"), "sub", "fsdp", None), P("parts", None), P("parts", None))
    return jax.shard_map(body, mesh=mesh, in_specs=in_specs, out_specs=out_specs, check_vma=False)
```

```python
import functools

import jax
import jax.numpy as jnp
from jax import lax
from jax.experimental import pallas as pl
from jax.experimental.pallas import tpu as pltpu
from jax.sharding import PartitionSpec as P

MBLK = 12
BF = jnp.bfloat16
F32 = jnp.float32
VMEM_LIMIT = 28 * 1024 * 1024


def params(**kw):
    return pltpu.CompilerParams(vmem_limit_bytes=VMEM_LIMIT, **kw)


def dg(a, b, ca, cb):
    return lax.dot_general(a, b, (((ca,), (cb,)), ((), ())), preferred_element_type=F32)


def places_of(storage, cols):
    ids = jnp.arange(storage.shape[0], dtype=jnp.int32)
    return jnp.sum(jnp.where(cols[..., None] == ids, storage, 0), axis=-1)


def ranks_in(mask):
    size = mask.shape[-1]
    before = jnp.arange(size)[:, None] > jnp.arange(size)[None, :]
    return jnp.sum(jnp.where(before, mask[..., None, :], 0), axis=-1)


def pack_kernel(src, interp, *outs):
    pairs, width = outs[0].shape[0], outs[0].shape[1]
    for h, out in enumerate(outs):
        for o in range(pairs):
            for c in range(width):
                out[o, c] = interp[src[o, h * width + c]]


def pack(src, values, pieces):
    pairs, width = src.shape[0], src.shape[1] // pieces
    block = values.shape[1]
    shape = (pairs, width, block, block)
    return pl.pallas_call(
        pack_kernel,
        grid_spec=pltpu.PrefetchScalarGridSpec(
            num_scalar_prefetch=1,
            grid=(1,),
            in_specs=[pl.BlockSpec(values.shape, lambda i, t: (0, 0, 0))],
            out_specs=[pl.BlockSpec(shape, lambda i, t: (0, 0, 0, 0))] * pieces,
        ),
        out_shape=[jax.ShapeDtypeStruct(shape, BF)] * pieces,
        compiler_params=params(),
        name="pack",
    )(src, values)


def forward_kernel(meta, x, w_in, a_down, a_up, w_out, *rest, nf, deps):
    embs, rest = rest[deps : deps + nf], rest[deps + nf :]
    normed, slope, inv, mid, hold = rest
    feats = x[...]
    middle = dg(a_down[...], feats, 0, 0).astype(BF)
    pre = dg(w_in[...], feats, 0, 0) + dg(a_up[...], middle, 0, 0)
    sig = jax.nn.sigmoid(pre)
    hidden = (pre * sig).astype(BF)
    slope[...] = sig * (1.0 + pre * (1.0 - sig))
    raw = dg(w_out[...], hidden, 0, 0)
    center = raw - jnp.mean(raw, axis=0, keepdims=True)
    istd = lax.rsqrt(jnp.mean(center * center, axis=0, keepdims=True) + 1e-05)
    norm = center * istd
    normed[...] = norm
    inv[...] = istd
    mid[...] = middle
    hold[...] = norm.astype(BF)
    chans = embs[0].shape[0]
    for r, emb in enumerate(embs):
        at = lax.rem(meta[0] + r, nf) * chans
        emb[...] = hold[pl.ds(pl.multiple_of(at, chans), chans), :]


def forward(meta, x, w_in, a_down, a_up, w_out, nf, deps):
    width, rows = w_out.shape[0], x.shape[1]
    rank = a_down.shape[1]
    step = min(512, rows)
    chans = width // nf
    full = lambda a: pl.BlockSpec(a.shape, lambda i, m: (0, 0))
    return pl.pallas_call(
        functools.partial(forward_kernel, nf=nf, deps=len(deps)),
        grid_spec=pltpu.PrefetchScalarGridSpec(
            num_scalar_prefetch=1,
            grid=(rows // step,),
            in_specs=[
                pl.BlockSpec((x.shape[0], step), lambda i, m: (0, i)),
                full(w_in),
                full(a_down),
                full(a_up),
                full(w_out),
            ]
            + [pl.BlockSpec(memory_space=pl.ANY)] * len(deps),
            out_specs=[pl.BlockSpec((chans, step), lambda i, m: (0, i))] * nf
            + [
                pl.BlockSpec((width, step), lambda i, m: (0, i)),
                pl.BlockSpec((width, step), lambda i, m: (0, i)),
                pl.BlockSpec((1, step), lambda i, m: (0, i)),
                pl.BlockSpec((rank, step), lambda i, m: (0, i)),
            ],
            scratch_shapes=[pltpu.VMEM((width, step), BF)],
        ),
        out_shape=[jax.ShapeDtypeStruct((chans, rows), BF)] * nf
        + [
            jax.ShapeDtypeStruct((width, rows), F32),
            jax.ShapeDtypeStruct((width, rows), F32),
            jax.ShapeDtypeStruct((1, rows), F32),
            jax.ShapeDtypeStruct((rank, rows), BF),
        ],
        compiler_params=params(),
        cost_estimate=pl.CostEstimate(
            flops=2 * rows * width * (width + x.shape[0]), bytes_accessed=rows * width * 12, transcendentals=0
        ),
        name="forward",
    )(meta, x, w_in, a_down, a_up, w_out, *deps)


def backward_kernel(offs, *refs, count):
    pieces = refs[:count]
    normed, slope, inv, mid, x, w_out, a_up, up, down, hold = refs[count:]
    chans = pieces[0].shape[0]
    for i, piece in enumerate(pieces):
        hold[pl.ds(pl.multiple_of(offs[i], chans), chans), :] = piece[...].astype(F32)
    e = hold[...]
    norm = normed[...]
    raw = inv[...] * (
        e
        - jnp.mean(e, axis=0, keepdims=True)
        - norm * jnp.mean(e * norm, axis=0, keepdims=True)
    )
    hidden_grad = dg(w_out[...], raw.astype(BF), 1, 0)
    pre_grad = (hidden_grad * slope[...]).astype(BF)
    up_term = dg(mid[...], pre_grad, 1, 1)
    mid_grad = dg(a_up[...], pre_grad, 1, 0).astype(BF)
    down_term = dg(mid_grad, x[...], 1, 1)

    @pl.when(pl.program_id(0) == 0)
    def _():
        up[...] = jnp.zeros_like(up)
        down[...] = jnp.zeros_like(down)

    up[...] += up_term
    down[...] += down_term


def backward(offs, pieces, normed, slope, inv, mid, x, w_out, a_up):
    width, rows = normed.shape
    rank = a_up.shape[0]
    step = min(512, rows)
    full = lambda a: pl.BlockSpec(a.shape, lambda i, m: (0, 0))
    tall = lambda a: pl.BlockSpec((a.shape[0], step), lambda i, m: (0, i))
    return pl.pallas_call(
        functools.partial(backward_kernel, count=len(pieces)),
        grid_spec=pltpu.PrefetchScalarGridSpec(
            num_scalar_prefetch=1,
            grid=(rows // step,),
            in_specs=[tall(p) for p in pieces]
            + [tall(normed), tall(slope), tall(inv), tall(mid), tall(x), full(w_out), full(a_up)],
            out_specs=[
                pl.BlockSpec((rank, width), lambda i, m: (0, 0)),
                pl.BlockSpec((rank, x.shape[0]), lambda i, m: (0, 0)),
            ],
            scratch_shapes=[pltpu.VMEM((width, step), F32)],
        ),
        out_shape=[
            jax.ShapeDtypeStruct((rank, width), F32),
            jax.ShapeDtypeStruct((rank, x.shape[0]), F32),
        ],
        compiler_params=params(),
        cost_estimate=pl.CostEstimate(
            flops=2 * rows * width * width, bytes_accessed=rows * width * 10, transcendentals=0
        ),
        name="backward",
    )(offs, *pieces, normed, slope, inv, mid, x, w_out, a_up)


def encode_kernel(tab_j, tab_m, meta, *refs, panels, weights, deps, n, ns, place, chunks):
    xs, ws = refs[:panels], refs[panels : panels + weights]
    refs = refs[: panels + weights] + refs[panels + weights + deps :]
    outs, rest = refs[panels + weights :][:chunks], refs[panels + weights + chunks :]
    acc = rest[0]
    r = pl.program_id(0)
    p = meta[place] * ns + r
    chans, block = outs[0].shape[2:]
    if panels > 1:
        hold = rest[1]
        wide = xs[0].shape[1]

        @pl.when(r == 0)
        def _():
            for i, piece in enumerate(xs):
                at = lax.rem(meta[n] + panels - i, panels) * wide
                hold[:, pl.ds(pl.multiple_of(at, wide), wide)] = piece[...]

        source = hold
    else:
        source = xs[0]
    acc[...] = jnp.zeros_like(acc)
    slot = 0
    for w in ws:
        for c in range(w.shape[1]):
            j, m = tab_j[p, slot], tab_m[p, slot]
            slot += 1
            panel = source[:, pl.ds(pl.multiple_of(j * block, block), block)]
            acc[m] += dg(panel, w[0, c], 1, 1)
    for k, out in enumerate(outs):
        out[0] = acc[0 : out.shape[1], k * chans : (k + 1) * chans].astype(BF)


def encode(tab_j, tab_m, meta, pieces, weights, deps, n, ns, place, chunks):
    chans, wide = pieces[0].shape
    panels = len(pieces)
    block = weights[0].shape[2]
    cap = sum(w.shape[1] for w in weights)
    scratch = [pltpu.VMEM((MBLK + 1, chans, block), F32)]
    if panels > 1:
        scratch.append(pltpu.VMEM((chans, wide * panels), BF))
    where = lambda r, j, m, t: (t[place] * ns + r, 0, 0, 0)
    return pl.pallas_call(
        functools.partial(
            encode_kernel, panels=panels, weights=len(weights), deps=len(deps), n=n, ns=ns,
            place=place, chunks=chunks,
        ),
        grid_spec=pltpu.PrefetchScalarGridSpec(
            num_scalar_prefetch=3,
            grid=(ns,),
            in_specs=[pl.BlockSpec((chans, wide), lambda r, j, m, t: (0, 0))] * panels
            + [pl.BlockSpec((1,) + w.shape[1:], where) for w in weights]
            + [pl.BlockSpec(memory_space=pl.ANY)] * len(deps),
            out_specs=[
                pl.BlockSpec((1, MBLK, chans // chunks, block), lambda r, j, m, t: (r, 0, 0, 0))
            ]
            * chunks,
            scratch_shapes=scratch,
        ),
        out_shape=[jax.ShapeDtypeStruct((ns, MBLK, chans // chunks, block), BF)] * chunks,
        compiler_params=params(),
        cost_estimate=pl.CostEstimate(
            flops=2 * ns * cap * chans * block * block * 4,
            bytes_accessed=ns * MBLK * chans * block * 4,
            transcendentals=0,
        ),
        name="encode",
    )(tab_j, tab_m, meta, *pieces, *weights, *deps)


def decode_kernel(tab_j, tab_m, meta, *refs, n, ns, weights, nf, chunks):
    each = 2 * n - 1
    count = each * chunks
    ws, rest = refs[count : count + weights], refs[count + weights :]
    outs, (hold, acc, sem) = rest[:-3], rest[-3:]
    z, s = meta[0], meta[1]
    chans, block = refs[0].shape[2:]
    for k in range(chunks):
        group = refs[k * each : (k + 1) * each]
        mine, theirs = group[:n], (None,) + group[n:]

        def copy(ref, r):
            to = hold.at[r, :, :, pl.ds(k * chans, chans), :]
            pltpu.make_async_copy(ref, to, sem.at[r, k]).start()

        copy(group[0], 0)
        for r in range(1, n):
            above = z + r < n
            for here, test in ((mine, 1), (theirs, 0)):

                @pl.when(jnp.logical_and(above, s == test))
                def _():
                    copy(here[r], r)

                @pl.when(jnp.logical_and(jnp.logical_not(above), s == 1 - test))
                def _():
                    copy(here[n - r], r)

    acc[...] = jnp.zeros_like(acc)

    def step(i, carry):
        for k in range(chunks):
            to = hold.at[i, :, :, pl.ds(k * chans, chans), :]
            pltpu.make_async_copy(refs[k * each], to, sem.at[i, k]).wait()
        for side in range(ns):
            p = lax.rem(z + i, n) * ns + side
            slot = 0
            for w in ws:
                for c in range(w.shape[1]):
                    j, m = tab_j[p, slot], tab_m[p, slot]
                    slot += 1
                    acc[j] += dg(hold[i, side, jnp.minimum(m, MBLK - 1)], w[p, c], 1, 0)
        return carry

    lax.fori_loop(0, n, step, 0)
    per = (acc.shape[0] - 1) // nf
    for r, out in enumerate(outs):
        first = lax.rem(meta[2] + r, nf) * per
        for g in range(per):
            out[:, g * block : (g + 1) * block] = acc[first + g].astype(BF)


def decode(tab_j, tab_m, meta, meshes, weights, grid_count, nf, n, ns, chunks):
    chans, block = meshes[0].shape[2] * chunks, meshes[0].shape[3]
    rows = grid_count * block
    shape = (chans, rows // nf)
    return pl.pallas_call(
        functools.partial(
            decode_kernel, n=n, ns=ns, weights=len(weights), nf=nf, chunks=chunks
        ),
        grid_spec=pltpu.PrefetchScalarGridSpec(
            num_scalar_prefetch=3,
            grid=(1,),
            in_specs=[pl.BlockSpec(memory_space=pl.ANY)] * len(meshes)
            + [pl.BlockSpec(w.shape, lambda i, j, m, t: (0, 0, 0, 0)) for w in weights],
            out_specs=[pl.BlockSpec(shape, lambda i, j, m, t: (0, 0))] * nf,
            scratch_shapes=[
                pltpu.VMEM((n, ns, MBLK, chans, block), BF),
                pltpu.VMEM((grid_count + 1, chans, block), F32),
                pltpu.SemaphoreType.DMA((n, chunks)),
            ],
        ),
        out_shape=[jax.ShapeDtypeStruct(shape, BF)] * nf,
        compiler_params=params(),
        cost_estimate=pl.CostEstimate(
            flops=2 * n * ns * 16 * chans * block * block * 4,
            bytes_accessed=2 * n * MBLK * chans * block * 4,
            transcendentals=0,
        ),
        name="decode",
    )(tab_j, tab_m, meta, *meshes, *weights)


def swap_sub(a):
    ns = lax.axis_size("sub")
    return lax.ppermute(a, "sub", [(i, (i + 1) % ns) for i in range(ns)])


def add_kernel(*refs, count):
    value = refs[0][...].astype(F32)
    for ref in refs[1:count]:
        value = value + ref[...].astype(F32)
    refs[-1][...] = value.astype(BF)


def add(terms, deps):
    shape = terms[0].shape
    parts = 3 if shape[1] % 3 == 0 else 1
    spec = pl.BlockSpec((1, shape[1] // parts) + shape[2:], lambda i, j: (i, j, 0, 0))
    return pl.pallas_call(
        functools.partial(add_kernel, count=len(terms)),
        grid=(shape[0], parts),
        in_specs=[spec] * len(terms) + [pl.BlockSpec(memory_space=pl.ANY)] * len(deps),
        out_specs=spec,
        out_shape=jax.ShapeDtypeStruct(shape, BF),
        compiler_params=params(),
        name="add",
    )(*terms, *deps)


def along(value, reach_up, reach_down):
    n, ns = lax.axis_size("lat"), lax.axis_size("sub")
    pairs = [(i * ns, (i + 1) * ns) for i in range(n - 1) if reach_up(i)]
    pairs += [(i * ns + 1, (i - 1) * ns + 1) for i in range(1, n) if reach_down(i)]
    return lax.ppermute(value, ("lat", "sub"), pairs)


def reduce_step(t, value):
    n = lax.axis_size("lat")
    return along(value, lambda i: i <= t - 1, lambda i: i >= n - t)


def spread_step(t, value):
    n = lax.axis_size("lat")
    return along(value, lambda i: i >= t - 1, lambda i: i <= n - t)


def add_all(value, axes):
    for axis in axes:
        size, step = lax.axis_size(axis), 1
        while step < size:
            value = value + lax.ppermute(value, axis, [(i, i ^ step) for i in range(size)])
            step *= 2
    return value


def body(
    grid_input_channels,
    cotangent,
    frozen_input_weight,
    frozen_output_weight,
    adapter_down_weight,
    adapter_up_weight,
    interp,
    nonzero_block_rows,
    nonzero_block_columns,
    grid_block_storage,
):
    n, ns = lax.axis_size("lat"), lax.axis_size("sub")
    nf, npart = lax.axis_size("fsdp"), lax.axis_size("parts")
    z, s = lax.axis_index("lat"), lax.axis_index("sub")
    f, y = lax.axis_index("fsdp"), lax.axis_index("parts")
    pairs = n * ns
    me = z * ns + s
    slots, block = interp.shape[2], interp.shape[3]
    chans, grid_rows = cotangent.shape[2], cotangent.shape[3]
    grid_count = grid_rows // block
    width = frozen_output_weight.shape[0]
    cap = max(2, (4 * slots + 3 * pairs - 1) // (3 * pairs))
    x = grid_input_channels.reshape(grid_input_channels.shape[2:])
    cot = cotangent.reshape(chans, grid_rows)
    values = interp.reshape(slots, block, block)
    storage = grid_block_storage.astype(jnp.int32)
    cols = nonzero_block_columns.reshape(slots)
    rows = nonzero_block_rows.reshape(slots)
    pair_ids = jnp.arange(pairs, dtype=jnp.int32)

    place = places_of(storage, cols)
    marks = (place[None, :] // grid_count == pair_ids[:, None]).astype(jnp.int32)
    rank = ranks_in(marks)
    shared = nf == 2 and npart == 2 and cap % 8 == 0
    if shared:
        r0 = y * 2 + f
        cs = cap // 4
        send_ranks = r0 * cs + jnp.arange(cs, dtype=jnp.int32)
    else:
        send_ranks = jnp.arange(cap, dtype=jnp.int32)
    hit = (rank[:, None, :] == send_ranks[None, :, None]) & (marks[:, None, :] > 0)
    src = jnp.sum(jnp.where(hit, jnp.arange(slots, dtype=jnp.int32), 0), axis=-1)
    a2a = lambda v: lax.all_to_all(v, ("lat", "sub"), 0, 0, tiled=True)
    meta_f = jnp.stack([f]).astype(jnp.int32)
    *emb, normed, slope, inv, mid = forward(
        meta_f, x, frozen_input_weight, adapter_down_weight, adapter_up_weight,
        frozen_output_weight, nf, [],
    )
    if shared:
        first, second = pack(src, values, 2)
        second, _ = lax.optimization_barrier((second, mid))
        first, second = a2a(first), a2a(second)
        flip = [(0, 1), (1, 0)]
        over_x = lambda v: lax.ppermute(v, "fsdp", flip)
        over_y = lambda v: lax.ppermute(v, "parts", flip)
        x1, y1, x2, y2 = over_x(first), over_y(first), over_x(second), over_y(second)
        weights = [first, second, x1, x2, y1, y2, over_x(y1), over_y(x2)]
        half = jnp.arange(cs, dtype=jnp.int32)
        slot_ranks = jnp.concatenate([(r0 ^ k) * cs + half for k in range(4)])
    else:
        weights = [a2a(pack(src, values, 1)[0])]
        slot_ranks = send_ranks

    pattern = jnp.stack([cols, rows])[None]
    if shared:
        pattern, _ = lax.optimization_barrier((pattern, first))
    both = lax.all_gather(pattern, ("lat", "sub"), tiled=True)
    every = places_of(storage, both[:, 0])
    mine = (every // grid_count == me).astype(jnp.int32)
    mine_rank = ranks_in(mine)
    hit = (mine_rank[:, None, :] == slot_ranks[None, :, None]) & (mine[:, None, :] > 0)
    found = jnp.any(hit, axis=-1)
    local = jnp.sum(jnp.where(hit, (every % grid_count)[:, None, :], 0), axis=-1)
    tab_m = jnp.where(found, jnp.sum(jnp.where(hit, both[:, 1][:, None, :], 0), axis=-1), MBLK)
    tab_get = jnp.where(found, local, 0)
    tab_put = jnp.where(found, local, grid_count)

    shift = lambda v, r: lax.ppermute(v, "fsdp", [(i, (i + r) % nf) for i in range(nf)])
    emb_pieces = [emb[r] if r == 0 else shift(emb[r], r) for r in range(nf)]

    meta_own = jnp.stack([z, s, f]).astype(jnp.int32)
    place_ids = jnp.arange(n, dtype=jnp.int32)
    away = jnp.where(s == 0, (n - place_ids) % n, place_ids)
    meta_enc = jnp.concatenate([(z + away) % n, f[None]]).astype(jnp.int32)

    chunks = 2
    halves = range(chunks)
    passes = [{"h": [{} for _ in halves]} for _ in range(2)]
    token = mid
    for now in range(3 * n - 1):
        for k, pieces in enumerate(([cot], emb_pieces)):
            whole, at = passes[k], now - n * k
            grad = k == 0

            def make(q, after):
                outs = encode(
                    tab_get, tab_m, meta_enc, pieces, weights, [after], n, ns, q, chunks
                )
                for h in halves:
                    whole["h"][h]["sums", q] = outs[h]

            if at == -1 or (at == 0 and grad):
                for q in (n - 1, 1):
                    make(q, token)
                for st in whole["h"]:
                    st["other", 1] = swap_sub(st["sums", n - 1])
            for h, st in enumerate(whole["h"]):
                ahead = passes[0]["h"][h]
                if 0 <= at < n - 1:
                    t = at + 1
                    behind = emb_pieces[1:] if t == n - 1 else []
                    behind = behind if grad else [ahead["came", t]]
                    terms = [st["sums", t], st["other", t]] + ([st["now"]] if t > 1 else [])
                    sent = add(terms, behind)
                    st["now"] = reduce_step(t, sent)
                    if h == chunks - 1:
                        if t == 1:
                            for q in range(n):
                                if q not in (1, n - 1):
                                    make(q, sent)
                            for other in whole["h"]:
                                for u in range(2, n):
                                    other["other", u] = swap_sub(other["sums", n - u])
                        if t == n - 1:
                            token = sent
                elif n - 1 <= at < 2 * n - 2:
                    t = at - n + 2
                    if t == 1:
                        behind = [] if grad else [passes[0]["out"][0]]
                        half = add([st["sums", 0], st["now"]], behind)
                        st["mesh"] = st["now"] = add([half, swap_sub(half)], [])
                    if not grad and t > 1 and h == chunks - 1:
                        if t == n - 1:
                            sums = backward(
                                offs, grads, normed, slope, inv, mid, x,
                                frozen_output_weight, adapter_up_weight,
                            )
                            sums = add_all(jnp.concatenate(sums, axis=1), ("sub", "fsdp"))
                        done = [sums] if t == n - 1 else grads
                        st["now"], *_ = lax.optimization_barrier((st["now"], *done))
                    st["now"] = st["came", t] = spread_step(t, st["now"])
                    st["theirs", t] = swap_sub(st["now"])
            if at == 2 * n - 2:
                meshes = []
                for st in whole["h"]:
                    meshes.append(st["mesh"])
                    meshes += [st["came", t] for t in range(1, n)]
                    meshes += [st["theirs", t] for t in range(1, n)]
                whole["out"] = decode(
                    tab_put, tab_m, meta_own, meshes, weights, grid_count, nf if grad else 1,
                    n, ns, chunks,
                )
                if grad:
                    grads = [shift(g, r) if r else g for r, g in enumerate(whole["out"])]
                    turns = jnp.arange(nf, dtype=jnp.int32)
                    offs = (((f - turns + nf) % nf) * chans).astype(jnp.int32)
    decoded = passes[1]["out"][0]

    sums = add_all(sums, ("lat",))
    up_gradient, grad_down = sums[:, :width], sums[:, width:].T
    return (decoded.reshape(1, 1, chans, grid_rows), grad_down, up_gradient)


def solution(mesh):
    in_specs = (
        P(("parts", "lat"), "sub", None, "fsdp"),
        P(("parts", "lat"), "sub", "fsdp", None),
        P(),
        P(),
        P("parts", None),
        P("parts", None),
        P("lat", "sub", None, None, None),
        P("lat", "sub", None),
        P("lat", "sub", None),
        P(),
    )
    out_specs = (P(("parts", "lat"), "sub", "fsdp", None), P("parts", None), P("parts", None))
    return jax.shard_map(body, mesh=mesh, in_specs=in_specs, out_specs=out_specs, check_vma=False)
```

```python
import functools

import jax
import jax.numpy as jnp
from jax import lax
from jax.experimental import pallas as pl
from jax.experimental.pallas import tpu as pltpu
from jax.sharding import PartitionSpec as P

MBLK = 12
BF = jnp.bfloat16
F32 = jnp.float32
VMEM_LIMIT = 28 * 1024 * 1024


def params(**kw):
    return pltpu.CompilerParams(vmem_limit_bytes=VMEM_LIMIT, **kw)


def dg(a, b, ca, cb):
    return lax.dot_general(a, b, (((ca,), (cb,)), ((), ())), preferred_element_type=F32)


def places_of(storage, cols):
    ids = jnp.arange(storage.shape[0], dtype=jnp.int32)
    return jnp.sum(jnp.where(cols[..., None] == ids, storage, 0), axis=-1)


def ranks_in(mask):
    size = mask.shape[-1]
    before = jnp.arange(size)[:, None] > jnp.arange(size)[None, :]
    return jnp.sum(jnp.where(before, mask[..., None, :], 0), axis=-1)


def pack_kernel(src, interp, *outs):
    pairs, width = outs[0].shape[0], outs[0].shape[1]
    for h, out in enumerate(outs):
        for o in range(pairs):
            for c in range(width):
                out[o, c] = interp[src[o, h * width + c]]


def pack(src, values, pieces):
    pairs, width = src.shape[0], src.shape[1] // pieces
    block = values.shape[1]
    shape = (pairs, width, block, block)
    return pl.pallas_call(
        pack_kernel,
        grid_spec=pltpu.PrefetchScalarGridSpec(
            num_scalar_prefetch=1,
            grid=(1,),
            in_specs=[pl.BlockSpec(values.shape, lambda i, t: (0, 0, 0))],
            out_specs=[pl.BlockSpec(shape, lambda i, t: (0, 0, 0, 0))] * pieces,
        ),
        out_shape=[jax.ShapeDtypeStruct(shape, BF)] * pieces,
        compiler_params=params(),
        name="pack",
    )(src, values)


def forward_kernel(meta, x, w_in, a_down, a_up, w_out, *rest, nf, deps):
    embs, rest = rest[deps : deps + nf], rest[deps + nf :]
    normed, slope, inv, mid, hold = rest
    feats = x[...]
    middle = dg(a_down[...], feats, 0, 0).astype(BF)
    pre = dg(w_in[...], feats, 0, 0) + dg(a_up[...], middle, 0, 0)
    sig = jax.nn.sigmoid(pre)
    hidden = (pre * sig).astype(BF)
    slope[...] = sig * (1.0 + pre * (1.0 - sig))
    raw = dg(w_out[...], hidden, 0, 0)
    center = raw - jnp.mean(raw, axis=0, keepdims=True)
    istd = lax.rsqrt(jnp.mean(center * center, axis=0, keepdims=True) + 1e-05)
    norm = center * istd
    normed[...] = norm
    inv[...] = istd
    mid[...] = middle
    hold[...] = norm.astype(BF)
    chans = embs[0].shape[0]
    for r, emb in enumerate(embs):
        at = lax.rem(meta[0] + r, nf) * chans
        emb[...] = hold[pl.ds(pl.multiple_of(at, chans), chans), :]


def forward(meta, x, w_in, a_down, a_up, w_out, nf, deps):
    width, rows = w_out.shape[0], x.shape[1]
    rank = a_down.shape[1]
    step = min(512, rows)
    chans = width // nf
    full = lambda a: pl.BlockSpec(a.shape, lambda i, m: (0, 0))
    return pl.pallas_call(
        functools.partial(forward_kernel, nf=nf, deps=len(deps)),
        grid_spec=pltpu.PrefetchScalarGridSpec(
            num_scalar_prefetch=1,
            grid=(rows // step,),
            in_specs=[
                pl.BlockSpec((x.shape[0], step), lambda i, m: (0, i)),
                full(w_in),
                full(a_down),
                full(a_up),
                full(w_out),
            ]
            + [pl.BlockSpec(memory_space=pl.ANY)] * len(deps),
            out_specs=[pl.BlockSpec((chans, step), lambda i, m: (0, i))] * nf
            + [
                pl.BlockSpec((width, step), lambda i, m: (0, i)),
                pl.BlockSpec((width, step), lambda i, m: (0, i)),
                pl.BlockSpec((1, step), lambda i, m: (0, i)),
                pl.BlockSpec((rank, step), lambda i, m: (0, i)),
            ],
            scratch_shapes=[pltpu.VMEM((width, step), BF)],
        ),
        out_shape=[jax.ShapeDtypeStruct((chans, rows), BF)] * nf
        + [
            jax.ShapeDtypeStruct((width, rows), F32),
            jax.ShapeDtypeStruct((width, rows), F32),
            jax.ShapeDtypeStruct((1, rows), F32),
            jax.ShapeDtypeStruct((rank, rows), BF),
        ],
        compiler_params=params(),
        cost_estimate=pl.CostEstimate(
            flops=2 * rows * width * (width + x.shape[0]), bytes_accessed=rows * width * 12, transcendentals=0
        ),
        name="forward",
    )(meta, x, w_in, a_down, a_up, w_out, *deps)


def backward_kernel(offs, *refs, count):
    pieces = refs[:count]
    normed, slope, inv, mid, x, w_out, a_up, up, down, hold = refs[count:]
    chans = pieces[0].shape[0]
    for i, piece in enumerate(pieces):
        hold[pl.ds(pl.multiple_of(offs[i], chans), chans), :] = piece[...].astype(F32)
    e = hold[...]
    norm = normed[...]
    raw = inv[...] * (
        e
        - jnp.mean(e, axis=0, keepdims=True)
        - norm * jnp.mean(e * norm, axis=0, keepdims=True)
    )
    hidden_grad = dg(w_out[...], raw.astype(BF), 1, 0)
    pre_grad = (hidden_grad * slope[...]).astype(BF)
    up_term = dg(mid[...], pre_grad, 1, 1)
    mid_grad = dg(a_up[...], pre_grad, 1, 0).astype(BF)
    down_term = dg(mid_grad, x[...], 1, 1)

    @pl.when(pl.program_id(0) == 0)
    def _():
        up[...] = jnp.zeros_like(up)
        down[...] = jnp.zeros_like(down)

    up[...] += up_term
    down[...] += down_term


def backward(offs, pieces, normed, slope, inv, mid, x, w_out, a_up):
    width, rows = normed.shape
    rank = a_up.shape[0]
    step = min(512, rows)
    full = lambda a: pl.BlockSpec(a.shape, lambda i, m: (0, 0))
    tall = lambda a: pl.BlockSpec((a.shape[0], step), lambda i, m: (0, i))
    return pl.pallas_call(
        functools.partial(backward_kernel, count=len(pieces)),
        grid_spec=pltpu.PrefetchScalarGridSpec(
            num_scalar_prefetch=1,
            grid=(rows // step,),
            in_specs=[tall(p) for p in pieces]
            + [tall(normed), tall(slope), tall(inv), tall(mid), tall(x), full(w_out), full(a_up)],
            out_specs=[
                pl.BlockSpec((rank, width), lambda i, m: (0, 0)),
                pl.BlockSpec((rank, x.shape[0]), lambda i, m: (0, 0)),
            ],
            scratch_shapes=[pltpu.VMEM((width, step), F32)],
        ),
        out_shape=[
            jax.ShapeDtypeStruct((rank, width), F32),
            jax.ShapeDtypeStruct((rank, x.shape[0]), F32),
        ],
        compiler_params=params(),
        cost_estimate=pl.CostEstimate(
            flops=2 * rows * width * width, bytes_accessed=rows * width * 10, transcendentals=0
        ),
        name="backward",
    )(offs, *pieces, normed, slope, inv, mid, x, w_out, a_up)


def encode_kernel(tab_j, tab_m, meta, *refs, panels, weights, deps, n, ns, place, chunks):
    xs, ws = refs[:panels], refs[panels : panels + weights]
    refs = refs[: panels + weights] + refs[panels + weights + deps :]
    outs, rest = refs[panels + weights :][:chunks], refs[panels + weights + chunks :]
    acc = rest[0]
    r = pl.program_id(0)
    p = meta[place] * ns + r
    chans, block = outs[0].shape[2:]
    if panels > 1:
        hold = rest[1]
        wide = xs[0].shape[1]

        @pl.when(r == 0)
        def _():
            for i, piece in enumerate(xs):
                at = lax.rem(meta[n] + panels - i, panels) * wide
                hold[:, pl.ds(pl.multiple_of(at, wide), wide)] = piece[...]

        source = hold
    else:
        source = xs[0]
    acc[...] = jnp.zeros_like(acc)
    slot = 0
    for w in ws:
        for c in range(w.shape[1]):
            j, m = tab_j[p, slot], tab_m[p, slot]
            slot += 1
            panel = source[:, pl.ds(pl.multiple_of(j * block, block), block)]
            acc[m] += dg(panel, w[0, c], 1, 1)
    for k, out in enumerate(outs):
        out[0] = acc[0 : out.shape[1], k * chans : (k + 1) * chans].astype(BF)


def encode(tab_j, tab_m, meta, pieces, weights, deps, n, ns, place, chunks):
    chans, wide = pieces[0].shape
    panels = len(pieces)
    block = weights[0].shape[2]
    cap = sum(w.shape[1] for w in weights)
    scratch = [pltpu.VMEM((MBLK + 1, chans, block), F32)]
    if panels > 1:
        scratch.append(pltpu.VMEM((chans, wide * panels), BF))
    where = lambda r, j, m, t: (t[place] * ns + r, 0, 0, 0)
    return pl.pallas_call(
        functools.partial(
            encode_kernel, panels=panels, weights=len(weights), deps=len(deps), n=n, ns=ns,
            place=place, chunks=chunks,
        ),
        grid_spec=pltpu.PrefetchScalarGridSpec(
            num_scalar_prefetch=3,
            grid=(ns,),
            in_specs=[pl.BlockSpec((chans, wide), lambda r, j, m, t: (0, 0))] * panels
            + [pl.BlockSpec((1,) + w.shape[1:], where) for w in weights]
            + [pl.BlockSpec(memory_space=pl.ANY)] * len(deps),
            out_specs=[
                pl.BlockSpec((1, MBLK, chans // chunks, block), lambda r, j, m, t: (r, 0, 0, 0))
            ]
            * chunks,
            scratch_shapes=scratch,
        ),
        out_shape=[jax.ShapeDtypeStruct((ns, MBLK, chans // chunks, block), BF)] * chunks,
        compiler_params=params(),
        cost_estimate=pl.CostEstimate(
            flops=2 * ns * cap * chans * block * block * 4,
            bytes_accessed=ns * MBLK * chans * block * 4,
            transcendentals=0,
        ),
        name="encode",
    )(tab_j, tab_m, meta, *pieces, *weights, *deps)


def decode_kernel(tab_j, tab_m, meta, *refs, n, ns, weights, nf, chunks):
    each = 2 * n - 1
    count = each * chunks
    ws, rest = refs[count : count + weights], refs[count + weights :]
    outs, (hold, acc, sem) = rest[:-3], rest[-3:]
    z, s = meta[0], meta[1]
    chans, block = refs[0].shape[2:]
    for k in range(chunks):
        group = refs[k * each : (k + 1) * each]
        mine, theirs = group[:n], (None,) + group[n:]

        def copy(ref, r):
            to = hold.at[r, :, :, pl.ds(k * chans, chans), :]
            pltpu.make_async_copy(ref, to, sem.at[r, k]).start()

        copy(group[0], 0)
        for r in range(1, n):
            above = z + r < n
            for here, test in ((mine, 1), (theirs, 0)):

                @pl.when(jnp.logical_and(above, s == test))
                def _():
                    copy(here[r], r)

                @pl.when(jnp.logical_and(jnp.logical_not(above), s == 1 - test))
                def _():
                    copy(here[n - r], r)

    acc[...] = jnp.zeros_like(acc)

    def step(i, carry):
        for k in range(chunks):
            to = hold.at[i, :, :, pl.ds(k * chans, chans), :]
            pltpu.make_async_copy(refs[k * each], to, sem.at[i, k]).wait()
        for side in range(ns):
            p = lax.rem(z + i, n) * ns + side
            slot = 0
            for w in ws:
                for c in range(w.shape[1]):
                    j, m = tab_j[p, slot], tab_m[p, slot]
                    slot += 1
                    acc[j] += dg(hold[i, side, jnp.minimum(m, MBLK - 1)], w[p, c], 1, 0)
        return carry

    lax.fori_loop(0, n, step, 0)
    per = (acc.shape[0] - 1) // nf
    for r, out in enumerate(outs):
        first = lax.rem(meta[2] + r, nf) * per
        for g in range(per):
            out[:, g * block : (g + 1) * block] = acc[first + g].astype(BF)


def decode(tab_j, tab_m, meta, meshes, weights, grid_count, nf, n, ns, chunks):
    chans, block = meshes[0].shape[2] * chunks, meshes[0].shape[3]
    rows = grid_count * block
    shape = (chans, rows // nf)
    return pl.pallas_call(
        functools.partial(
            decode_kernel, n=n, ns=ns, weights=len(weights), nf=nf, chunks=chunks
        ),
        grid_spec=pltpu.PrefetchScalarGridSpec(
            num_scalar_prefetch=3,
            grid=(1,),
            in_specs=[pl.BlockSpec(memory_space=pl.ANY)] * len(meshes)
            + [pl.BlockSpec(w.shape, lambda i, j, m, t: (0, 0, 0, 0)) for w in weights],
            out_specs=[pl.BlockSpec(shape, lambda i, j, m, t: (0, 0))] * nf,
            scratch_shapes=[
                pltpu.VMEM((n, ns, MBLK, chans, block), BF),
                pltpu.VMEM((grid_count + 1, chans, block), F32),
                pltpu.SemaphoreType.DMA((n, chunks)),
            ],
        ),
        out_shape=[jax.ShapeDtypeStruct(shape, BF)] * nf,
        compiler_params=params(),
        cost_estimate=pl.CostEstimate(
            flops=2 * n * ns * 16 * chans * block * block * 4,
            bytes_accessed=2 * n * MBLK * chans * block * 4,
            transcendentals=0,
        ),
        name="decode",
    )(tab_j, tab_m, meta, *meshes, *weights)


def swap_sub(a):
    ns = lax.axis_size("sub")
    return lax.ppermute(a, "sub", [(i, (i + 1) % ns) for i in range(ns)])


def add_kernel(*refs, count):
    value = refs[0][...].astype(F32)
    for ref in refs[1:count]:
        value = value + ref[...].astype(F32)
    refs[-1][...] = value.astype(BF)


def add(terms, deps):
    shape = terms[0].shape
    parts = 3 if shape[1] % 3 == 0 else 1
    spec = pl.BlockSpec((1, shape[1] // parts) + shape[2:], lambda i, j: (i, j, 0, 0))
    return pl.pallas_call(
        functools.partial(add_kernel, count=len(terms)),
        grid=(shape[0], parts),
        in_specs=[spec] * len(terms) + [pl.BlockSpec(memory_space=pl.ANY)] * len(deps),
        out_specs=spec,
        out_shape=jax.ShapeDtypeStruct(shape, BF),
        compiler_params=params(),
        name="add",
    )(*terms, *deps)


def along(value, reach_up, reach_down):
    n, ns = lax.axis_size("lat"), lax.axis_size("sub")
    pairs = [(i * ns, (i + 1) * ns) for i in range(n - 1) if reach_up(i)]
    pairs += [(i * ns + 1, (i - 1) * ns + 1) for i in range(1, n) if reach_down(i)]
    return lax.ppermute(value, ("lat", "sub"), pairs)


def reduce_step(t, value):
    n = lax.axis_size("lat")
    return along(value, lambda i: i <= t - 1, lambda i: i >= n - t)


def spread_step(t, value):
    n = lax.axis_size("lat")
    return along(value, lambda i: i >= t - 1, lambda i: i <= n - t)


def add_all(value, axes):
    for axis in axes:
        size, step = lax.axis_size(axis), 1
        while step < size:
            value = value + lax.ppermute(value, axis, [(i, i ^ step) for i in range(size)])
            step *= 2
    return value


def body(
    grid_input_channels,
    cotangent,
    frozen_input_weight,
    frozen_output_weight,
    adapter_down_weight,
    adapter_up_weight,
    interp,
    nonzero_block_rows,
    nonzero_block_columns,
    grid_block_storage,
):
    n, ns = lax.axis_size("lat"), lax.axis_size("sub")
    nf, npart = lax.axis_size("fsdp"), lax.axis_size("parts")
    z, s = lax.axis_index("lat"), lax.axis_index("sub")
    f, y = lax.axis_index("fsdp"), lax.axis_index("parts")
    pairs = n * ns
    me = z * ns + s
    slots, block = interp.shape[2], interp.shape[3]
    chans, grid_rows = cotangent.shape[2], cotangent.shape[3]
    grid_count = grid_rows // block
    width = frozen_output_weight.shape[0]
    cap = max(2, (4 * slots + 3 * pairs - 1) // (3 * pairs))
    x = grid_input_channels.reshape(grid_input_channels.shape[2:])
    cot = cotangent.reshape(chans, grid_rows)
    values = interp.reshape(slots, block, block)
    storage = grid_block_storage.astype(jnp.int32)
    cols = nonzero_block_columns.reshape(slots)
    rows = nonzero_block_rows.reshape(slots)
    pair_ids = jnp.arange(pairs, dtype=jnp.int32)

    place = places_of(storage, cols)
    marks = (place[None, :] // grid_count == pair_ids[:, None]).astype(jnp.int32)
    rank = ranks_in(marks)
    shared = nf == 2 and npart == 2 and cap % 8 == 0
    if shared:
        r0 = y * 2 + f
        cs = cap // 4
        send_ranks = r0 * cs + jnp.arange(cs, dtype=jnp.int32)
    else:
        send_ranks = jnp.arange(cap, dtype=jnp.int32)
    hit = (rank[:, None, :] == send_ranks[None, :, None]) & (marks[:, None, :] > 0)
    src = jnp.sum(jnp.where(hit, jnp.arange(slots, dtype=jnp.int32), 0), axis=-1)
    a2a = lambda v: lax.all_to_all(v, ("lat", "sub"), 0, 0, tiled=True)
    meta_f = jnp.stack([f]).astype(jnp.int32)
    *emb, normed, slope, inv, mid = forward(
        meta_f, x, frozen_input_weight, adapter_down_weight, adapter_up_weight,
        frozen_output_weight, nf, [],
    )
    if shared:
        first, second = pack(src, values, 2)
        second, _ = lax.optimization_barrier((second, mid))
        first, second = a2a(first), a2a(second)
        flip = [(0, 1), (1, 0)]
        over_x = lambda v: lax.ppermute(v, "fsdp", flip)
        over_y = lambda v: lax.ppermute(v, "parts", flip)
        x1, y1, x2, y2 = over_x(first), over_y(first), over_x(second), over_y(second)
        weights = [first, second, x1, x2, y1, y2, over_x(y1), over_y(x2)]
        half = jnp.arange(cs, dtype=jnp.int32)
        slot_ranks = jnp.concatenate([(r0 ^ k) * cs + half for k in range(4)])
    else:
        weights = [a2a(pack(src, values, 1)[0])]
        slot_ranks = send_ranks

    pattern = jnp.stack([cols, rows])[None]
    if shared:
        pattern, _ = lax.optimization_barrier((pattern, first))
    both = lax.all_gather(pattern, ("lat", "sub"), tiled=True)
    every = places_of(storage, both[:, 0])
    mine = (every // grid_count == me).astype(jnp.int32)
    mine_rank = ranks_in(mine)
    hit = (mine_rank[:, None, :] == slot_ranks[None, :, None]) & (mine[:, None, :] > 0)
    found = jnp.any(hit, axis=-1)
    local = jnp.sum(jnp.where(hit, (every % grid_count)[:, None, :], 0), axis=-1)
    tab_m = jnp.where(found, jnp.sum(jnp.where(hit, both[:, 1][:, None, :], 0), axis=-1), MBLK)
    tab_get = jnp.where(found, local, 0)
    tab_put = jnp.where(found, local, grid_count)

    shift = lambda v, r: lax.ppermute(v, "fsdp", [(i, (i + r) % nf) for i in range(nf)])
    emb_pieces = [emb[r] if r == 0 else shift(emb[r], r) for r in range(nf)]

    meta_own = jnp.stack([z, s, f]).astype(jnp.int32)
    place_ids = jnp.arange(n, dtype=jnp.int32)
    away = jnp.where(s == 0, (n - place_ids) % n, place_ids)
    meta_enc = jnp.concatenate([(z + away) % n, f[None]]).astype(jnp.int32)

    chunks = 2
    halves = range(chunks)
    passes = [{"h": [{} for _ in halves]} for _ in range(2)]
    token = mid
    for now in range(3 * n - 1):
        for k, pieces in enumerate(([cot], emb_pieces)):
            whole, at = passes[k], now - n * k
            grad = k == 0

            def make(q, after):
                outs = encode(
                    tab_get, tab_m, meta_enc, pieces, weights, [after], n, ns, q, chunks
                )
                for h in halves:
                    whole["h"][h]["sums", q] = outs[h]

            if at == -1 or (at == 0 and grad):
                for q in (n - 1, 1):
                    make(q, token)
                for st in whole["h"]:
                    st["other", 1] = swap_sub(st["sums", n - 1])
            for h, st in enumerate(whole["h"]):
                ahead = passes[0]["h"][h]
                if 0 <= at < n - 1:
                    t = at + 1
                    behind = emb_pieces[1:] if t == n - 1 else []
                    behind = behind if grad else [ahead["came", t]]
                    terms = [st["sums", t], st["other", t]] + ([st["now"]] if t > 1 else [])
                    sent = add(terms, behind)
                    st["now"] = reduce_step(t, sent)
                    if h == chunks - 1:
                        if t == 1:
                            for q in range(n):
                                if q not in (1, n - 1):
                                    make(q, sent)
                            for other in whole["h"]:
                                for u in range(2, n):
                                    other["other", u] = swap_sub(other["sums", n - u])
                        if t == n - 1:
                            token = sent
                elif n - 1 <= at < 2 * n - 2:
                    t = at - n + 2
                    if t == 1:
                        behind = [] if grad else [passes[0]["out"][0]]
                        half = add([st["sums", 0], st["now"]], behind)
                        st["mesh"] = st["now"] = add([half, swap_sub(half)], [])
                    if not grad and t == n - 1 and h == chunks - 1:
                        if t == n - 1:
                            sums = backward(
                                offs, grads, normed, slope, inv, mid, x,
                                frozen_output_weight, adapter_up_weight,
                            )
                            sums = add_all(jnp.concatenate(sums, axis=1), ("sub", "fsdp", "lat"))
                        done = [sums]
                        st["now"], *_ = lax.optimization_barrier((st["now"], *done))
                    st["now"] = st["came", t] = spread_step(t, st["now"])
                    st["theirs", t] = swap_sub(st["now"])
            if at == 2 * n - 2:
                meshes = []
                for st in whole["h"]:
                    meshes.append(st["mesh"])
                    meshes += [st["came", t] for t in range(1, n)]
                    meshes += [st["theirs", t] for t in range(1, n)]
                whole["out"] = decode(
                    tab_put, tab_m, meta_own, meshes, weights, grid_count, nf if grad else 1,
                    n, ns, chunks,
                )
                if grad:
                    grads = [shift(g, r) if r else g for r, g in enumerate(whole["out"])]
                    turns = jnp.arange(nf, dtype=jnp.int32)
                    offs = (((f - turns + nf) % nf) * chans).astype(jnp.int32)
    decoded = passes[1]["out"][0]

    up_gradient, grad_down = sums[:, :width], sums[:, width:].T
    return (decoded.reshape(1, 1, chans, grid_rows), grad_down, up_gradient)


def solution(mesh):
    in_specs = (
        P(("parts", "lat"), "sub", None, "fsdp"),
        P(("parts", "lat"), "sub", "fsdp", None),
        P(),
        P(),
        P("parts", None),
        P("parts", None),
        P("lat", "sub", None, None, None),
        P("lat", "sub", None),
        P("lat", "sub", None),
        P(),
    )
    out_specs = (P(("parts", "lat"), "sub", "fsdp", None), P("parts", None), P("parts", None))
    return jax.shard_map(body, mesh=mesh, in_specs=in_specs, out_specs=out_specs, check_vma=False)
```

```python
import functools

import jax
import jax.numpy as jnp
from jax import lax
from jax.experimental import pallas as pl
from jax.experimental.pallas import tpu as pltpu
from jax.sharding import PartitionSpec as P

MBLK = 12
BF = jnp.bfloat16
F32 = jnp.float32
VMEM_LIMIT = 28 * 1024 * 1024


def params(**kw):
    return pltpu.CompilerParams(vmem_limit_bytes=VMEM_LIMIT, **kw)


def dg(a, b, ca, cb):
    return lax.dot_general(a, b, (((ca,), (cb,)), ((), ())), preferred_element_type=F32)


def places_of(storage, cols):
    ids = jnp.arange(storage.shape[0], dtype=jnp.int32)
    return jnp.sum(jnp.where(cols[..., None] == ids, storage, 0), axis=-1)


def ranks_in(mask):
    size = mask.shape[-1]
    before = jnp.arange(size)[:, None] > jnp.arange(size)[None, :]
    return jnp.sum(jnp.where(before, mask[..., None, :], 0), axis=-1)


def pack_kernel(src, interp, *outs):
    pairs, width = outs[0].shape[0], outs[0].shape[1]
    for h, out in enumerate(outs):
        for o in range(pairs):
            for c in range(width):
                out[o, c] = interp[src[o, h * width + c]]


def pack(src, values, pieces):
    pairs, width = src.shape[0], src.shape[1] // pieces
    block = values.shape[1]
    shape = (pairs, width, block, block)
    return pl.pallas_call(
        pack_kernel,
        grid_spec=pltpu.PrefetchScalarGridSpec(
            num_scalar_prefetch=1,
            grid=(1,),
            in_specs=[pl.BlockSpec(values.shape, lambda i, t: (0, 0, 0))],
            out_specs=[pl.BlockSpec(shape, lambda i, t: (0, 0, 0, 0))] * pieces,
        ),
        out_shape=[jax.ShapeDtypeStruct(shape, BF)] * pieces,
        compiler_params=params(),
        name="pack",
    )(src, values)


def forward_kernel(meta, x, w_in, a_down, a_up, w_out, *rest, nf, deps):
    embs, rest = rest[deps : deps + nf], rest[deps + nf :]
    normed, slope, inv, mid, hold = rest
    feats = x[...]
    middle = dg(a_down[...], feats, 0, 0).astype(BF)
    pre = dg(w_in[...], feats, 0, 0) + dg(a_up[...], middle, 0, 0)
    sig = jax.nn.sigmoid(pre)
    hidden = (pre * sig).astype(BF)
    slope[...] = sig * (1.0 + pre * (1.0 - sig))
    raw = dg(w_out[...], hidden, 0, 0)
    center = raw - jnp.mean(raw, axis=0, keepdims=True)
    istd = lax.rsqrt(jnp.mean(center * center, axis=0, keepdims=True) + 1e-05)
    norm = center * istd
    normed[...] = norm
    inv[...] = istd
    mid[...] = middle
    hold[...] = norm.astype(BF)
    chans = embs[0].shape[0]
    for r, emb in enumerate(embs):
        at = lax.rem(meta[0] + r, nf) * chans
        emb[...] = hold[pl.ds(pl.multiple_of(at, chans), chans), :]


def forward(meta, x, w_in, a_down, a_up, w_out, nf, deps):
    width, rows = w_out.shape[0], x.shape[1]
    rank = a_down.shape[1]
    step = min(512, rows)
    chans = width // nf
    full = lambda a: pl.BlockSpec(a.shape, lambda i, m: (0, 0))
    return pl.pallas_call(
        functools.partial(forward_kernel, nf=nf, deps=len(deps)),
        grid_spec=pltpu.PrefetchScalarGridSpec(
            num_scalar_prefetch=1,
            grid=(rows // step,),
            in_specs=[
                pl.BlockSpec((x.shape[0], step), lambda i, m: (0, i)),
                full(w_in),
                full(a_down),
                full(a_up),
                full(w_out),
            ]
            + [pl.BlockSpec(memory_space=pl.ANY)] * len(deps),
            out_specs=[pl.BlockSpec((chans, step), lambda i, m: (0, i))] * nf
            + [
                pl.BlockSpec((width, step), lambda i, m: (0, i)),
                pl.BlockSpec((width, step), lambda i, m: (0, i)),
                pl.BlockSpec((1, step), lambda i, m: (0, i)),
                pl.BlockSpec((rank, step), lambda i, m: (0, i)),
            ],
            scratch_shapes=[pltpu.VMEM((width, step), BF)],
        ),
        out_shape=[jax.ShapeDtypeStruct((chans, rows), BF)] * nf
        + [
            jax.ShapeDtypeStruct((width, rows), F32),
            jax.ShapeDtypeStruct((width, rows), F32),
            jax.ShapeDtypeStruct((1, rows), F32),
            jax.ShapeDtypeStruct((rank, rows), BF),
        ],
        compiler_params=params(),
        cost_estimate=pl.CostEstimate(
            flops=2 * rows * width * (width + x.shape[0]), bytes_accessed=rows * width * 12, transcendentals=0
        ),
        name="forward",
    )(meta, x, w_in, a_down, a_up, w_out, *deps)


def backward_kernel(offs, *refs, count):
    pieces = refs[:count]
    normed, slope, inv, mid, x, w_out, a_up, up, down, hold = refs[count:]
    chans = pieces[0].shape[0]
    for i, piece in enumerate(pieces):
        hold[pl.ds(pl.multiple_of(offs[i], chans), chans), :] = piece[...].astype(F32)
    e = hold[...]
    norm = normed[...]
    raw = inv[...] * (
        e
        - jnp.mean(e, axis=0, keepdims=True)
        - norm * jnp.mean(e * norm, axis=0, keepdims=True)
    )
    hidden_grad = dg(w_out[...], raw.astype(BF), 1, 0)
    pre_grad = (hidden_grad * slope[...]).astype(BF)
    up_term = dg(mid[...], pre_grad, 1, 1)
    mid_grad = dg(a_up[...], pre_grad, 1, 0).astype(BF)
    down_term = dg(mid_grad, x[...], 1, 1)

    @pl.when(pl.program_id(0) == 0)
    def _():
        up[...] = jnp.zeros_like(up)
        down[...] = jnp.zeros_like(down)

    up[...] += up_term
    down[...] += down_term


def backward(offs, pieces, normed, slope, inv, mid, x, w_out, a_up):
    width, rows = normed.shape
    rank = a_up.shape[0]
    step = min(512, rows)
    full = lambda a: pl.BlockSpec(a.shape, lambda i, m: (0, 0))
    tall = lambda a: pl.BlockSpec((a.shape[0], step), lambda i, m: (0, i))
    return pl.pallas_call(
        functools.partial(backward_kernel, count=len(pieces)),
        grid_spec=pltpu.PrefetchScalarGridSpec(
            num_scalar_prefetch=1,
            grid=(rows // step,),
            in_specs=[tall(p) for p in pieces]
            + [tall(normed), tall(slope), tall(inv), tall(mid), tall(x), full(w_out), full(a_up)],
            out_specs=[
                pl.BlockSpec((rank, width), lambda i, m: (0, 0)),
                pl.BlockSpec((rank, x.shape[0]), lambda i, m: (0, 0)),
            ],
            scratch_shapes=[pltpu.VMEM((width, step), F32)],
        ),
        out_shape=[
            jax.ShapeDtypeStruct((rank, width), F32),
            jax.ShapeDtypeStruct((rank, x.shape[0]), F32),
        ],
        compiler_params=params(),
        cost_estimate=pl.CostEstimate(
            flops=2 * rows * width * width, bytes_accessed=rows * width * 10, transcendentals=0
        ),
        name="backward",
    )(offs, *pieces, normed, slope, inv, mid, x, w_out, a_up)


def encode_kernel(tab_j, tab_m, meta, *refs, panels, weights, deps, n, ns, place, chunks):
    xs, ws = refs[:panels], refs[panels : panels + weights]
    refs = refs[: panels + weights] + refs[panels + weights + deps :]
    outs, rest = refs[panels + weights :][:chunks], refs[panels + weights + chunks :]
    acc = rest[0]
    r = pl.program_id(0)
    p = meta[place] * ns + r
    chans, block = outs[0].shape[2:]
    if panels > 1:
        hold = rest[1]
        wide = xs[0].shape[1]

        @pl.when(r == 0)
        def _():
            for i, piece in enumerate(xs):
                at = lax.rem(meta[n] + panels - i, panels) * wide
                hold[:, pl.ds(pl.multiple_of(at, wide), wide)] = piece[...]

        source = hold
    else:
        source = xs[0]
    acc[...] = jnp.zeros_like(acc)
    slot = 0
    for w in ws:
        for c in range(w.shape[1]):
            j, m = tab_j[p, slot], tab_m[p, slot]
            slot += 1
            panel = source[:, pl.ds(pl.multiple_of(j * block, block), block)]
            acc[m] += dg(panel, w[0, c], 1, 1)
    for k, out in enumerate(outs):
        out[0] = acc[0 : out.shape[1], k * chans : (k + 1) * chans].astype(BF)


def encode(tab_j, tab_m, meta, pieces, weights, deps, n, ns, place, chunks):
    chans, wide = pieces[0].shape
    panels = len(pieces)
    block = weights[0].shape[2]
    cap = sum(w.shape[1] for w in weights)
    scratch = [pltpu.VMEM((MBLK + 1, chans, block), F32)]
    if panels > 1:
        scratch.append(pltpu.VMEM((chans, wide * panels), BF))
    where = lambda r, j, m, t: (t[place] * ns + r, 0, 0, 0)
    return pl.pallas_call(
        functools.partial(
            encode_kernel, panels=panels, weights=len(weights), deps=len(deps), n=n, ns=ns,
            place=place, chunks=chunks,
        ),
        grid_spec=pltpu.PrefetchScalarGridSpec(
            num_scalar_prefetch=3,
            grid=(ns,),
            in_specs=[pl.BlockSpec((chans, wide), lambda r, j, m, t: (0, 0))] * panels
            + [pl.BlockSpec((1,) + w.shape[1:], where) for w in weights]
            + [pl.BlockSpec(memory_space=pl.ANY)] * len(deps),
            out_specs=[
                pl.BlockSpec((1, MBLK, chans // chunks, block), lambda r, j, m, t: (r, 0, 0, 0))
            ]
            * chunks,
            scratch_shapes=scratch,
        ),
        out_shape=[jax.ShapeDtypeStruct((ns, MBLK, chans // chunks, block), BF)] * chunks,
        compiler_params=params(),
        cost_estimate=pl.CostEstimate(
            flops=2 * ns * cap * chans * block * block * 4,
            bytes_accessed=ns * MBLK * chans * block * 4,
            transcendentals=0,
        ),
        name="encode",
    )(tab_j, tab_m, meta, *pieces, *weights, *deps)


def decode_kernel(tab_j, tab_m, meta, *refs, n, ns, weights, nf, chunks):
    each = 2 * n - 1
    count = each * chunks
    ws, rest = refs[count : count + weights], refs[count + weights :]
    outs, (hold, acc, sem) = rest[:-3], rest[-3:]
    z, s = meta[0], meta[1]
    chans, block = refs[0].shape[2:]
    for k in range(chunks):
        group = refs[k * each : (k + 1) * each]
        mine, theirs = group[:n], (None,) + group[n:]

        def copy(ref, r):
            to = hold.at[r, :, :, pl.ds(k * chans, chans), :]
            pltpu.make_async_copy(ref, to, sem.at[r, k]).start()

        copy(group[0], 0)
        for r in range(1, n):
            above = z + r < n
            for here, test in ((mine, 1), (theirs, 0)):

                @pl.when(jnp.logical_and(above, s == test))
                def _():
                    copy(here[r], r)

                @pl.when(jnp.logical_and(jnp.logical_not(above), s == 1 - test))
                def _():
                    copy(here[n - r], r)

    acc[...] = jnp.zeros_like(acc)

    def step(i, carry):
        for k in range(chunks):
            to = hold.at[i, :, :, pl.ds(k * chans, chans), :]
            pltpu.make_async_copy(refs[k * each], to, sem.at[i, k]).wait()
        for side in range(ns):
            p = lax.rem(z + i, n) * ns + side
            slot = 0
            for w in ws:
                for c in range(w.shape[1]):
                    j, m = tab_j[p, slot], tab_m[p, slot]
                    slot += 1
                    acc[j] += dg(hold[i, side, jnp.minimum(m, MBLK - 1)], w[p, c], 1, 0)
        return carry

    lax.fori_loop(0, n, step, 0)
    per = (acc.shape[0] - 1) // nf
    for r, out in enumerate(outs):
        first = lax.rem(meta[2] + r, nf) * per
        for g in range(per):
            out[:, g * block : (g + 1) * block] = acc[first + g].astype(BF)


def decode(tab_j, tab_m, meta, meshes, weights, grid_count, nf, n, ns, chunks):
    chans, block = meshes[0].shape[2] * chunks, meshes[0].shape[3]
    rows = grid_count * block
    shape = (chans, rows // nf)
    return pl.pallas_call(
        functools.partial(
            decode_kernel, n=n, ns=ns, weights=len(weights), nf=nf, chunks=chunks
        ),
        grid_spec=pltpu.PrefetchScalarGridSpec(
            num_scalar_prefetch=3,
            grid=(1,),
            in_specs=[pl.BlockSpec(memory_space=pl.ANY)] * len(meshes)
            + [pl.BlockSpec(w.shape, lambda i, j, m, t: (0, 0, 0, 0)) for w in weights],
            out_specs=[pl.BlockSpec(shape, lambda i, j, m, t: (0, 0))] * nf,
            scratch_shapes=[
                pltpu.VMEM((n, ns, MBLK, chans, block), BF),
                pltpu.VMEM((grid_count + 1, chans, block), F32),
                pltpu.SemaphoreType.DMA((n, chunks)),
            ],
        ),
        out_shape=[jax.ShapeDtypeStruct(shape, BF)] * nf,
        compiler_params=params(),
        cost_estimate=pl.CostEstimate(
            flops=2 * n * ns * 16 * chans * block * block * 4,
            bytes_accessed=2 * n * MBLK * chans * block * 4,
            transcendentals=0,
        ),
        name="decode",
    )(tab_j, tab_m, meta, *meshes, *weights)


def swap_sub(a):
    ns = lax.axis_size("sub")
    return lax.ppermute(a, "sub", [(i, (i + 1) % ns) for i in range(ns)])


def add_kernel(*refs, count):
    value = refs[0][...].astype(F32)
    for ref in refs[1:count]:
        value = value + ref[...].astype(F32)
    refs[-1][...] = value.astype(BF)


def add(terms, deps):
    shape = terms[0].shape
    parts = 3 if shape[1] % 3 == 0 else 1
    spec = pl.BlockSpec((1, shape[1] // parts) + shape[2:], lambda i, j: (i, j, 0, 0))
    return pl.pallas_call(
        functools.partial(add_kernel, count=len(terms)),
        grid=(shape[0], parts),
        in_specs=[spec] * len(terms) + [pl.BlockSpec(memory_space=pl.ANY)] * len(deps),
        out_specs=spec,
        out_shape=jax.ShapeDtypeStruct(shape, BF),
        compiler_params=params(),
        name="add",
    )(*terms, *deps)


def along(value, reach_up, reach_down):
    n, ns = lax.axis_size("lat"), lax.axis_size("sub")
    pairs = [(i * ns, (i + 1) * ns) for i in range(n - 1) if reach_up(i)]
    pairs += [(i * ns + 1, (i - 1) * ns + 1) for i in range(1, n) if reach_down(i)]
    return lax.ppermute(value, ("lat", "sub"), pairs)


def reduce_step(t, value):
    n = lax.axis_size("lat")
    return along(value, lambda i: i <= t - 1, lambda i: i >= n - t)


def spread_step(t, value):
    n = lax.axis_size("lat")
    return along(value, lambda i: i >= t - 1, lambda i: i <= n - t)


def add_all(value, axes):
    for axis in axes:
        size, step = lax.axis_size(axis), 1
        while step < size:
            value = value + lax.ppermute(value, axis, [(i, i ^ step) for i in range(size)])
            step *= 2
    return value


def body(
    grid_input_channels,
    cotangent,
    frozen_input_weight,
    frozen_output_weight,
    adapter_down_weight,
    adapter_up_weight,
    interp,
    nonzero_block_rows,
    nonzero_block_columns,
    grid_block_storage,
):
    n, ns = lax.axis_size("lat"), lax.axis_size("sub")
    nf, npart = lax.axis_size("fsdp"), lax.axis_size("parts")
    z, s = lax.axis_index("lat"), lax.axis_index("sub")
    f, y = lax.axis_index("fsdp"), lax.axis_index("parts")
    pairs = n * ns
    me = z * ns + s
    slots, block = interp.shape[2], interp.shape[3]
    chans, grid_rows = cotangent.shape[2], cotangent.shape[3]
    grid_count = grid_rows // block
    width = frozen_output_weight.shape[0]
    cap = max(2, (4 * slots + 3 * pairs - 1) // (3 * pairs))
    x = grid_input_channels.reshape(grid_input_channels.shape[2:])
    cot = cotangent.reshape(chans, grid_rows)
    values = interp.reshape(slots, block, block)
    storage = grid_block_storage.astype(jnp.int32)
    cols = nonzero_block_columns.reshape(slots)
    rows = nonzero_block_rows.reshape(slots)
    pair_ids = jnp.arange(pairs, dtype=jnp.int32)

    place = places_of(storage, cols)
    marks = (place[None, :] // grid_count == pair_ids[:, None]).astype(jnp.int32)
    rank = ranks_in(marks)
    shared = nf == 2 and npart == 2 and cap % 8 == 0
    if shared:
        r0 = y * 2 + f
        cs = cap // 4
        send_ranks = r0 * cs + jnp.arange(cs, dtype=jnp.int32)
    else:
        send_ranks = jnp.arange(cap, dtype=jnp.int32)
    hit = (rank[:, None, :] == send_ranks[None, :, None]) & (marks[:, None, :] > 0)
    src = jnp.sum(jnp.where(hit, jnp.arange(slots, dtype=jnp.int32), 0), axis=-1)
    a2a = lambda v: lax.all_to_all(v, ("lat", "sub"), 0, 0, tiled=True)
    meta_f = jnp.stack([f]).astype(jnp.int32)
    *emb, normed, slope, inv, mid = forward(
        meta_f, x, frozen_input_weight, adapter_down_weight, adapter_up_weight,
        frozen_output_weight, nf, [],
    )
    if shared:
        first, second = pack(src, values, 2)
        second, _ = lax.optimization_barrier((second, mid))
        first, second = a2a(first), a2a(second)
        flip = [(0, 1), (1, 0)]
        over_x = lambda v: lax.ppermute(v, "fsdp", flip)
        over_y = lambda v: lax.ppermute(v, "parts", flip)
        cut = cs // 4
        corner = lambda a, b: (over_x(b[:, :cut]), over_y(a[:, cut:]))
        x1, y1, x2, y2 = over_x(first), over_y(first), over_x(second), over_y(second)
        weights = [first, second, x1, x2, y1, y2, *corner(x1, y1), *corner(x2, y2)]
        half = jnp.arange(cs, dtype=jnp.int32)
        slot_ranks = jnp.concatenate([(r0 ^ k) * cs + half for k in range(4)])
    else:
        weights = [a2a(pack(src, values, 1)[0])]
        slot_ranks = send_ranks

    pattern = jnp.stack([cols, rows])[None]
    if shared:
        pattern, _ = lax.optimization_barrier((pattern, first))
    both = lax.all_gather(pattern, ("lat", "sub"), tiled=True)
    every = places_of(storage, both[:, 0])
    mine = (every // grid_count == me).astype(jnp.int32)
    mine_rank = ranks_in(mine)
    hit = (mine_rank[:, None, :] == slot_ranks[None, :, None]) & (mine[:, None, :] > 0)
    found = jnp.any(hit, axis=-1)
    local = jnp.sum(jnp.where(hit, (every % grid_count)[:, None, :], 0), axis=-1)
    tab_m = jnp.where(found, jnp.sum(jnp.where(hit, both[:, 1][:, None, :], 0), axis=-1), MBLK)
    tab_get = jnp.where(found, local, 0)
    tab_put = jnp.where(found, local, grid_count)

    shift = lambda v, r: lax.ppermute(v, "fsdp", [(i, (i + r) % nf) for i in range(nf)])
    emb_pieces = [emb[r] if r == 0 else shift(emb[r], r) for r in range(nf)]

    meta_own = jnp.stack([z, s, f]).astype(jnp.int32)
    place_ids = jnp.arange(n, dtype=jnp.int32)
    away = jnp.where(s == 0, (n - place_ids) % n, place_ids)
    meta_enc = jnp.concatenate([(z + away) % n, f[None]]).astype(jnp.int32)

    chunks = 2
    halves = range(chunks)
    passes = [{"h": [{} for _ in halves]} for _ in range(2)]
    token = mid
    for now in range(3 * n - 1):
        for k, pieces in enumerate(([cot], emb_pieces)):
            whole, at = passes[k], now - n * k
            grad = k == 0

            def make(q, after):
                outs = encode(
                    tab_get, tab_m, meta_enc, pieces, weights, [after], n, ns, q, chunks
                )
                for h in halves:
                    whole["h"][h]["sums", q] = outs[h]

            if at == -1 or (at == 0 and grad):
                for q in (n - 1, 1):
                    make(q, token)
                for st in whole["h"]:
                    st["other", 1] = swap_sub(st["sums", n - 1])
            for h, st in enumerate(whole["h"]):
                ahead = passes[0]["h"][h]
                if 0 <= at < n - 1:
                    t = at + 1
                    behind = emb_pieces[1:] if t == n - 1 else []
                    behind = behind if grad else [ahead["came", t]]
                    terms = [st["sums", t], st["other", t]] + ([st["now"]] if t > 1 else [])
                    sent = add(terms, behind)
                    st["now"] = reduce_step(t, sent)
                    if h == chunks - 1:
                        if t == 1:
                            for q in range(n):
                                if q not in (1, n - 1):
                                    make(q, sent)
                            for other in whole["h"]:
                                for u in range(2, n):
                                    other["other", u] = swap_sub(other["sums", n - u])
                        if t == n - 1:
                            token = sent
                elif n - 1 <= at < 2 * n - 2:
                    t = at - n + 2
                    if t == 1:
                        behind = [] if grad else [passes[0]["out"][0]]
                        half = add([st["sums", 0], st["now"]], behind)
                        st["mesh"] = st["now"] = add([half, swap_sub(half)], [])
                    if not grad and t == n - 1 and h == chunks - 1:
                        if t == n - 1:
                            sums = backward(
                                offs, grads, normed, slope, inv, mid, x,
                                frozen_output_weight, adapter_up_weight,
                            )
                            sums = add_all(jnp.concatenate(sums, axis=1), ("sub", "fsdp", "lat"))
                        done = [sums]
                        st["now"], *_ = lax.optimization_barrier((st["now"], *done))
                    st["now"] = st["came", t] = spread_step(t, st["now"])
                    st["theirs", t] = swap_sub(st["now"])
            if at == 2 * n - 2:
                meshes = []
                for st in whole["h"]:
                    meshes.append(st["mesh"])
                    meshes += [st["came", t] for t in range(1, n)]
                    meshes += [st["theirs", t] for t in range(1, n)]
                whole["out"] = decode(
                    tab_put, tab_m, meta_own, meshes, weights, grid_count, nf if grad else 1,
                    n, ns, chunks,
                )
                if grad:
                    grads = [shift(g, r) if r else g for r, g in enumerate(whole["out"])]
                    turns = jnp.arange(nf, dtype=jnp.int32)
                    offs = (((f - turns + nf) % nf) * chans).astype(jnp.int32)
    decoded = passes[1]["out"][0]

    up_gradient, grad_down = sums[:, :width], sums[:, width:].T
    return (decoded.reshape(1, 1, chans, grid_rows), grad_down, up_gradient)


def solution(mesh):
    in_specs = (
        P(("parts", "lat"), "sub", None, "fsdp"),
        P(("parts", "lat"), "sub", "fsdp", None),
        P(),
        P(),
        P("parts", None),
        P("parts", None),
        P("lat", "sub", None, None, None),
        P("lat", "sub", None),
        P("lat", "sub", None),
        P(),
    )
    out_specs = (P(("parts", "lat"), "sub", "fsdp", None), P("parts", None), P("parts", None))
    return jax.shard_map(body, mesh=mesh, in_specs=in_specs, out_specs=out_specs, check_vma=False)
```

```python
import functools

import jax
import jax.numpy as jnp
from jax import lax
from jax.experimental import pallas as pl
from jax.experimental.pallas import tpu as pltpu
from jax.sharding import PartitionSpec as P

MBLK = 12
BF = jnp.bfloat16
F32 = jnp.float32
VMEM_LIMIT = 28 * 1024 * 1024


def params(**kw):
    return pltpu.CompilerParams(vmem_limit_bytes=VMEM_LIMIT, **kw)


def dg(a, b, ca, cb):
    return lax.dot_general(a, b, (((ca,), (cb,)), ((), ())), preferred_element_type=F32)


def places_of(storage, cols):
    ids = jnp.arange(storage.shape[0], dtype=jnp.int32)
    return jnp.sum(jnp.where(cols[..., None] == ids, storage, 0), axis=-1)


def ranks_in(mask):
    size = mask.shape[-1]
    before = jnp.arange(size)[:, None] > jnp.arange(size)[None, :]
    return jnp.sum(jnp.where(before, mask[..., None, :], 0), axis=-1)


def pack_kernel(src, interp, *outs):
    pairs, width = outs[0].shape[0], outs[0].shape[1]
    for h, out in enumerate(outs):
        for o in range(pairs):
            for c in range(width):
                out[o, c] = interp[src[o, h * width + c]]


def pack(src, values, pieces):
    pairs, width = src.shape[0], src.shape[1] // pieces
    block = values.shape[1]
    shape = (pairs, width, block, block)
    return pl.pallas_call(
        pack_kernel,
        grid_spec=pltpu.PrefetchScalarGridSpec(
            num_scalar_prefetch=1,
            grid=(1,),
            in_specs=[pl.BlockSpec(values.shape, lambda i, t: (0, 0, 0))],
            out_specs=[pl.BlockSpec(shape, lambda i, t: (0, 0, 0, 0))] * pieces,
        ),
        out_shape=[jax.ShapeDtypeStruct(shape, BF)] * pieces,
        compiler_params=params(),
        name="pack",
    )(src, values)


def forward_kernel(meta, x, w_in, a_down, a_up, w_out, *rest, nf, deps):
    embs, rest = rest[deps : deps + nf], rest[deps + nf :]
    normed, slope, inv, mid, hold = rest
    feats = x[...]
    middle = dg(a_down[...], feats, 0, 0).astype(BF)
    pre = dg(w_in[...], feats, 0, 0) + dg(a_up[...], middle, 0, 0)
    sig = jax.nn.sigmoid(pre)
    hidden = (pre * sig).astype(BF)
    slope[...] = sig * (1.0 + pre * (1.0 - sig))
    raw = dg(w_out[...], hidden, 0, 0)
    center = raw - jnp.mean(raw, axis=0, keepdims=True)
    istd = lax.rsqrt(jnp.mean(center * center, axis=0, keepdims=True) + 1e-05)
    norm = center * istd
    normed[...] = norm
    inv[...] = istd
    mid[...] = middle
    hold[...] = norm.astype(BF)
    chans = embs[0].shape[0]
    for r, emb in enumerate(embs):
        at = lax.rem(meta[0] + r, nf) * chans
        emb[...] = hold[pl.ds(pl.multiple_of(at, chans), chans), :]


def forward(meta, x, w_in, a_down, a_up, w_out, nf, deps):
    width, rows = w_out.shape[0], x.shape[1]
    rank = a_down.shape[1]
    step = min(1024, rows)
    chans = width // nf
    full = lambda a: pl.BlockSpec(a.shape, lambda i, m: (0, 0))
    return pl.pallas_call(
        functools.partial(forward_kernel, nf=nf, deps=len(deps)),
        grid_spec=pltpu.PrefetchScalarGridSpec(
            num_scalar_prefetch=1,
            grid=(rows // step,),
            in_specs=[
                pl.BlockSpec((x.shape[0], step), lambda i, m: (0, i)),
                full(w_in),
                full(a_down),
                full(a_up),
                full(w_out),
            ]
            + [pl.BlockSpec(memory_space=pl.ANY)] * len(deps),
            out_specs=[pl.BlockSpec((chans, step), lambda i, m: (0, i))] * nf
            + [
                pl.BlockSpec((width, step), lambda i, m: (0, i)),
                pl.BlockSpec((width, step), lambda i, m: (0, i)),
                pl.BlockSpec((1, step), lambda i, m: (0, i)),
                pl.BlockSpec((rank, step), lambda i, m: (0, i)),
            ],
            scratch_shapes=[pltpu.VMEM((width, step), BF)],
        ),
        out_shape=[jax.ShapeDtypeStruct((chans, rows), BF)] * nf
        + [
            jax.ShapeDtypeStruct((width, rows), F32),
            jax.ShapeDtypeStruct((width, rows), F32),
            jax.ShapeDtypeStruct((1, rows), F32),
            jax.ShapeDtypeStruct((rank, rows), BF),
        ],
        compiler_params=params(),
        cost_estimate=pl.CostEstimate(
            flops=2 * rows * width * (width + x.shape[0]), bytes_accessed=rows * width * 12, transcendentals=0
        ),
        name="forward",
    )(meta, x, w_in, a_down, a_up, w_out, *deps)


def backward_kernel(offs, *refs, count):
    pieces = refs[:count]
    normed, slope, inv, mid, x, w_out, a_up, up, down, hold = refs[count:]
    chans = pieces[0].shape[0]
    for i, piece in enumerate(pieces):
        hold[pl.ds(pl.multiple_of(offs[i], chans), chans), :] = piece[...].astype(F32)
    e = hold[...]
    norm = normed[...]
    raw = inv[...] * (
        e
        - jnp.mean(e, axis=0, keepdims=True)
        - norm * jnp.mean(e * norm, axis=0, keepdims=True)
    )
    hidden_grad = dg(w_out[...], raw.astype(BF), 1, 0)
    pre_grad = (hidden_grad * slope[...]).astype(BF)
    up_term = dg(mid[...], pre_grad, 1, 1)
    mid_grad = dg(a_up[...], pre_grad, 1, 0).astype(BF)
    down_term = dg(mid_grad, x[...], 1, 1)

    @pl.when(pl.program_id(0) == 0)
    def _():
        up[...] = jnp.zeros_like(up)
        down[...] = jnp.zeros_like(down)

    up[...] += up_term
    down[...] += down_term


def backward(offs, pieces, normed, slope, inv, mid, x, w_out, a_up):
    width, rows = normed.shape
    rank = a_up.shape[0]
    step = min(1024, rows)
    full = lambda a: pl.BlockSpec(a.shape, lambda i, m: (0, 0))
    tall = lambda a: pl.BlockSpec((a.shape[0], step), lambda i, m: (0, i))
    return pl.pallas_call(
        functools.partial(backward_kernel, count=len(pieces)),
        grid_spec=pltpu.PrefetchScalarGridSpec(
            num_scalar_prefetch=1,
            grid=(rows // step,),
            in_specs=[tall(p) for p in pieces]
            + [tall(normed), tall(slope), tall(inv), tall(mid), tall(x), full(w_out), full(a_up)],
            out_specs=[
                pl.BlockSpec((rank, width), lambda i, m: (0, 0)),
                pl.BlockSpec((rank, x.shape[0]), lambda i, m: (0, 0)),
            ],
            scratch_shapes=[pltpu.VMEM((width, step), F32)],
        ),
        out_shape=[
            jax.ShapeDtypeStruct((rank, width), F32),
            jax.ShapeDtypeStruct((rank, x.shape[0]), F32),
        ],
        compiler_params=params(),
        cost_estimate=pl.CostEstimate(
            flops=2 * rows * width * width, bytes_accessed=rows * width * 10, transcendentals=0
        ),
        name="backward",
    )(offs, *pieces, normed, slope, inv, mid, x, w_out, a_up)


def encode_kernel(tab_j, tab_m, meta, *refs, panels, weights, deps, n, ns, place, chunks):
    xs, ws = refs[:panels], refs[panels : panels + weights]
    refs = refs[: panels + weights] + refs[panels + weights + deps :]
    outs, rest = refs[panels + weights :][:chunks], refs[panels + weights + chunks :]
    acc = rest[0]
    r = pl.program_id(0)
    p = meta[place] * ns + r
    chans, block = outs[0].shape[2:]
    if panels > 1:
        hold = rest[1]
        wide = xs[0].shape[1]

        @pl.when(r == 0)
        def _():
            for i, piece in enumerate(xs):
                at = lax.rem(meta[n] + panels - i, panels) * wide
                hold[:, pl.ds(pl.multiple_of(at, wide), wide)] = piece[...]

        source = hold
    else:
        source = xs[0]
    acc[...] = jnp.zeros_like(acc)
    slot = 0
    for w in ws:
        for c in range(w.shape[1]):
            j, m = tab_j[p, slot], tab_m[p, slot]
            slot += 1
            panel = source[:, pl.ds(pl.multiple_of(j * block, block), block)]
            acc[m] += dg(panel, w[0, c], 1, 1)
    for k, out in enumerate(outs):
        out[0] = acc[0 : out.shape[1], k * chans : (k + 1) * chans].astype(BF)


def encode(tab_j, tab_m, meta, pieces, weights, deps, n, ns, place, chunks):
    chans, wide = pieces[0].shape
    panels = len(pieces)
    block = weights[0].shape[2]
    cap = sum(w.shape[1] for w in weights)
    scratch = [pltpu.VMEM((MBLK + 1, chans, block), F32)]
    if panels > 1:
        scratch.append(pltpu.VMEM((chans, wide * panels), BF))
    where = lambda r, j, m, t: (t[place] * ns + r, 0, 0, 0)
    return pl.pallas_call(
        functools.partial(
            encode_kernel, panels=panels, weights=len(weights), deps=len(deps), n=n, ns=ns,
            place=place, chunks=chunks,
        ),
        grid_spec=pltpu.PrefetchScalarGridSpec(
            num_scalar_prefetch=3,
            grid=(ns,),
            in_specs=[pl.BlockSpec((chans, wide), lambda r, j, m, t: (0, 0))] * panels
            + [pl.BlockSpec((1,) + w.shape[1:], where) for w in weights]
            + [pl.BlockSpec(memory_space=pl.ANY)] * len(deps),
            out_specs=[
                pl.BlockSpec((1, MBLK, chans // chunks, block), lambda r, j, m, t: (r, 0, 0, 0))
            ]
            * chunks,
            scratch_shapes=scratch,
        ),
        out_shape=[jax.ShapeDtypeStruct((ns, MBLK, chans // chunks, block), BF)] * chunks,
        compiler_params=params(),
        cost_estimate=pl.CostEstimate(
            flops=2 * ns * cap * chans * block * block * 4,
            bytes_accessed=ns * MBLK * chans * block * 4,
            transcendentals=0,
        ),
        name="encode",
    )(tab_j, tab_m, meta, *pieces, *weights, *deps)


def decode_kernel(tab_j, tab_m, meta, *refs, n, ns, weights, nf, chunks):
    each = 2 * n - 1
    count = each * chunks
    ws, rest = refs[count : count + weights], refs[count + weights :]
    outs, (hold, acc, sem) = rest[:-3], rest[-3:]
    z, s = meta[0], meta[1]
    chans, block = refs[0].shape[2:]
    for k in range(chunks):
        group = refs[k * each : (k + 1) * each]
        mine, theirs = group[:n], (None,) + group[n:]

        def copy(ref, r):
            to = hold.at[r, :, :, pl.ds(k * chans, chans), :]
            pltpu.make_async_copy(ref, to, sem.at[r, k]).start()

        copy(group[0], 0)
        for r in range(1, n):
            above = z + r < n
            for here, test in ((mine, 1), (theirs, 0)):

                @pl.when(jnp.logical_and(above, s == test))
                def _():
                    copy(here[r], r)

                @pl.when(jnp.logical_and(jnp.logical_not(above), s == 1 - test))
                def _():
                    copy(here[n - r], r)

    acc[...] = jnp.zeros_like(acc)

    def step(i, carry):
        for k in range(chunks):
            to = hold.at[i, :, :, pl.ds(k * chans, chans), :]
            pltpu.make_async_copy(refs[k * each], to, sem.at[i, k]).wait()
        for side in range(ns):
            p = lax.rem(z + i, n) * ns + side
            slot = 0
            for w in ws:
                for c in range(w.shape[1]):
                    j, m = tab_j[p, slot], tab_m[p, slot]
                    slot += 1
                    acc[j] += dg(hold[i, side, jnp.minimum(m, MBLK - 1)], w[p, c], 1, 0)
        return carry

    lax.fori_loop(0, n, step, 0)
    per = (acc.shape[0] - 1) // nf
    for r, out in enumerate(outs):
        first = lax.rem(meta[2] + r, nf) * per
        for g in range(per):
            out[:, g * block : (g + 1) * block] = acc[first + g].astype(BF)


def decode(tab_j, tab_m, meta, meshes, weights, grid_count, nf, n, ns, chunks):
    chans, block = meshes[0].shape[2] * chunks, meshes[0].shape[3]
    rows = grid_count * block
    shape = (chans, rows // nf)
    return pl.pallas_call(
        functools.partial(
            decode_kernel, n=n, ns=ns, weights=len(weights), nf=nf, chunks=chunks
        ),
        grid_spec=pltpu.PrefetchScalarGridSpec(
            num_scalar_prefetch=3,
            grid=(1,),
            in_specs=[pl.BlockSpec(memory_space=pl.ANY)] * len(meshes)
            + [pl.BlockSpec(w.shape, lambda i, j, m, t: (0, 0, 0, 0)) for w in weights],
            out_specs=[pl.BlockSpec(shape, lambda i, j, m, t: (0, 0))] * nf,
            scratch_shapes=[
                pltpu.VMEM((n, ns, MBLK, chans, block), BF),
                pltpu.VMEM((grid_count + 1, chans, block), F32),
                pltpu.SemaphoreType.DMA((n, chunks)),
            ],
        ),
        out_shape=[jax.ShapeDtypeStruct(shape, BF)] * nf,
        compiler_params=params(),
        cost_estimate=pl.CostEstimate(
            flops=2 * n * ns * 16 * chans * block * block * 4,
            bytes_accessed=2 * n * MBLK * chans * block * 4,
            transcendentals=0,
        ),
        name="decode",
    )(tab_j, tab_m, meta, *meshes, *weights)


def swap_sub(a):
    ns = lax.axis_size("sub")
    return lax.ppermute(a, "sub", [(i, (i + 1) % ns) for i in range(ns)])


def add_kernel(*refs, count):
    value = refs[0][...].astype(F32)
    for ref in refs[1:count]:
        value = value + ref[...].astype(F32)
    refs[-1][...] = value.astype(BF)


def add(terms, deps):
    shape = terms[0].shape
    parts = 1
    spec = pl.BlockSpec((1, shape[1] // parts) + shape[2:], lambda i, j: (i, j, 0, 0))
    return pl.pallas_call(
        functools.partial(add_kernel, count=len(terms)),
        grid=(shape[0], parts),
        in_specs=[spec] * len(terms) + [pl.BlockSpec(memory_space=pl.ANY)] * len(deps),
        out_specs=spec,
        out_shape=jax.ShapeDtypeStruct(shape, BF),
        compiler_params=params(),
        name="add",
    )(*terms, *deps)


def along(value, reach_up, reach_down):
    n, ns = lax.axis_size("lat"), lax.axis_size("sub")
    pairs = [(i * ns, (i + 1) * ns) for i in range(n - 1) if reach_up(i)]
    pairs += [(i * ns + 1, (i - 1) * ns + 1) for i in range(1, n) if reach_down(i)]
    return lax.ppermute(value, ("lat", "sub"), pairs)


def reduce_step(t, value):
    n = lax.axis_size("lat")
    return along(value, lambda i: i <= t - 1, lambda i: i >= n - t)


def spread_step(t, value):
    n = lax.axis_size("lat")
    return along(value, lambda i: i >= t - 1, lambda i: i <= n - t)


def add_all(value, axes):
    for axis in axes:
        size, step = lax.axis_size(axis), 1
        while step < size:
            value = value + lax.ppermute(value, axis, [(i, i ^ step) for i in range(size)])
            step *= 2
    return value


def body(
    grid_input_channels,
    cotangent,
    frozen_input_weight,
    frozen_output_weight,
    adapter_down_weight,
    adapter_up_weight,
    interp,
    nonzero_block_rows,
    nonzero_block_columns,
    grid_block_storage,
):
    n, ns = lax.axis_size("lat"), lax.axis_size("sub")
    nf, npart = lax.axis_size("fsdp"), lax.axis_size("parts")
    z, s = lax.axis_index("lat"), lax.axis_index("sub")
    f, y = lax.axis_index("fsdp"), lax.axis_index("parts")
    pairs = n * ns
    me = z * ns + s
    slots, block = interp.shape[2], interp.shape[3]
    chans, grid_rows = cotangent.shape[2], cotangent.shape[3]
    grid_count = grid_rows // block
    width = frozen_output_weight.shape[0]
    cap = max(2, (4 * slots + 3 * pairs - 1) // (3 * pairs))
    x = grid_input_channels.reshape(grid_input_channels.shape[2:])
    cot = cotangent.reshape(chans, grid_rows)
    values = interp.reshape(slots, block, block)
    storage = grid_block_storage.astype(jnp.int32)
    cols = nonzero_block_columns.reshape(slots)
    rows = nonzero_block_rows.reshape(slots)
    pair_ids = jnp.arange(pairs, dtype=jnp.int32)

    place = places_of(storage, cols)
    marks = (place[None, :] // grid_count == pair_ids[:, None]).astype(jnp.int32)
    rank = ranks_in(marks)
    shared = nf == 2 and npart == 2 and cap % 8 == 0
    if shared:
        r0 = y * 2 + f
        cs = cap // 4
        send_ranks = r0 * cs + jnp.arange(cs, dtype=jnp.int32)
    else:
        send_ranks = jnp.arange(cap, dtype=jnp.int32)
    hit = (rank[:, None, :] == send_ranks[None, :, None]) & (marks[:, None, :] > 0)
    src = jnp.sum(jnp.where(hit, jnp.arange(slots, dtype=jnp.int32), 0), axis=-1)
    a2a = lambda v: lax.all_to_all(v, ("lat", "sub"), 0, 0, tiled=True)
    meta_f = jnp.stack([f]).astype(jnp.int32)
    *emb, normed, slope, inv, mid = forward(
        meta_f, x, frozen_input_weight, adapter_down_weight, adapter_up_weight,
        frozen_output_weight, nf, [],
    )
    if shared:
        first, second = pack(src, values, 2)
        second, _ = lax.optimization_barrier((second, mid))
        first, second = a2a(first), a2a(second)
        flip = [(0, 1), (1, 0)]
        over_x = lambda v: lax.ppermute(v, "fsdp", flip)
        over_y = lambda v: lax.ppermute(v, "parts", flip)
        cut = cs // 4
        corner = lambda a, b: (over_x(b[:, :cut]), over_y(a[:, cut:]))
        x1, y1, x2, y2 = over_x(first), over_y(first), over_x(second), over_y(second)
        weights = [first, second, x1, x2, y1, y2, *corner(x1, y1), *corner(x2, y2)]
        half = jnp.arange(cs, dtype=jnp.int32)
        slot_ranks = jnp.concatenate([(r0 ^ k) * cs + half for k in range(4)])
    else:
        weights = [a2a(pack(src, values, 1)[0])]
        slot_ranks = send_ranks

    pattern = jnp.stack([cols, rows])[None]
    if shared:
        pattern, _ = lax.optimization_barrier((pattern, first))
    both = lax.all_gather(pattern, ("lat", "sub"), tiled=True)
    every = places_of(storage, both[:, 0])
    mine = (every // grid_count == me).astype(jnp.int32)
    mine_rank = ranks_in(mine)
    hit = (mine_rank[:, None, :] == slot_ranks[None, :, None]) & (mine[:, None, :] > 0)
    found = jnp.any(hit, axis=-1)
    local = jnp.sum(jnp.where(hit, (every % grid_count)[:, None, :], 0), axis=-1)
    tab_m = jnp.where(found, jnp.sum(jnp.where(hit, both[:, 1][:, None, :], 0), axis=-1), MBLK)
    tab_get = jnp.where(found, local, 0)
    tab_put = jnp.where(found, local, grid_count)

    shift = lambda v, r: lax.ppermute(v, "fsdp", [(i, (i + r) % nf) for i in range(nf)])
    emb_pieces = [emb[r] if r == 0 else shift(emb[r], r) for r in range(nf)]

    meta_own = jnp.stack([z, s, f]).astype(jnp.int32)
    place_ids = jnp.arange(n, dtype=jnp.int32)
    away = jnp.where(s == 0, (n - place_ids) % n, place_ids)
    meta_enc = jnp.concatenate([(z + away) % n, f[None]]).astype(jnp.int32)

    chunks = 2
    halves = range(chunks)
    passes = [{"h": [{} for _ in halves]} for _ in range(2)]
    token = mid
    for now in range(3 * n - 1):
        for k, pieces in enumerate(([cot], emb_pieces)):
            whole, at = passes[k], now - n * k
            grad = k == 0

            def make(q, after):
                outs = encode(
                    tab_get, tab_m, meta_enc, pieces, weights, [after], n, ns, q, chunks
                )
                for h in halves:
                    whole["h"][h]["sums", q] = outs[h]

            if at == -1 or (at == 0 and grad):
                for q in (n - 1, 1):
                    make(q, token)
                for st in whole["h"]:
                    st["other", 1] = swap_sub(st["sums", n - 1])
            for h, st in enumerate(whole["h"]):
                ahead = passes[0]["h"][h]
                if 0 <= at < n - 1:
                    t = at + 1
                    behind = emb_pieces[1:] if t == n - 1 else []
                    behind = behind if grad else [ahead["came", t]]
                    terms = [st["sums", t], st["other", t]] + ([st["now"]] if t > 1 else [])
                    sent = add(terms, behind)
                    st["now"] = reduce_step(t, sent)
                    if h == chunks - 1:
                        if t == 1:
                            for q in range(n):
                                if q not in (1, n - 1):
                                    make(q, sent)
                            for other in whole["h"]:
                                for u in range(2, n):
                                    other["other", u] = swap_sub(other["sums", n - u])
                        if t == n - 1:
                            token = sent
                elif n - 1 <= at < 2 * n - 2:
                    t = at - n + 2
                    if t == 1:
                        behind = [] if grad else [passes[0]["out"][0]]
                        half = add([st["sums", 0], st["now"]], behind)
                        st["mesh"] = st["now"] = add([half, swap_sub(half)], [])
                    if not grad and t == n - 1 and h == chunks - 1:
                        if t == n - 1:
                            sums = backward(
                                offs, grads, normed, slope, inv, mid, x,
                                frozen_output_weight, adapter_up_weight,
                            )
                            sums = add_all(jnp.concatenate(sums, axis=1), ("sub", "fsdp", "lat"))
                        done = [sums]
                        st["now"], *_ = lax.optimization_barrier((st["now"], *done))
                    st["now"] = st["came", t] = spread_step(t, st["now"])
                    st["theirs", t] = swap_sub(st["now"])
            if at == 2 * n - 2:
                meshes = []
                for st in whole["h"]:
                    meshes.append(st["mesh"])
                    meshes += [st["came", t] for t in range(1, n)]
                    meshes += [st["theirs", t] for t in range(1, n)]
                whole["out"] = decode(
                    tab_put, tab_m, meta_own, meshes, weights, grid_count, nf if grad else 1,
                    n, ns, chunks,
                )
                if grad:
                    grads = [shift(g, r) if r else g for r, g in enumerate(whole["out"])]
                    turns = jnp.arange(nf, dtype=jnp.int32)
                    offs = (((f - turns + nf) % nf) * chans).astype(jnp.int32)
    decoded = passes[1]["out"][0]

    up_gradient, grad_down = sums[:, :width], sums[:, width:].T
    return (decoded.reshape(1, 1, chans, grid_rows), grad_down, up_gradient)


def solution(mesh):
    in_specs = (
        P(("parts", "lat"), "sub", None, "fsdp"),
        P(("parts", "lat"), "sub", "fsdp", None),
        P(),
        P(),
        P("parts", None),
        P("parts", None),
        P("lat", "sub", None, None, None),
        P("lat", "sub", None),
        P("lat", "sub", None),
        P(),
    )
    out_specs = (P(("parts", "lat"), "sub", "fsdp", None), P("parts", None), P("parts", None))
    return jax.shard_map(body, mesh=mesh, in_specs=in_specs, out_specs=out_specs, check_vma=False)
```
